128 devices in a mesh: dp: 8 (over x, z_lo), seq: 16 (over y, z_hi, core).
Axes of the slice: x: 4, y: 4, z: 4 (z_hi: 2, z_lo: 2; z = z_hi * 2 + z_lo), core: 2. Of those that a mesh axis runs over, the one named last changes fastest.
Arguments:
- tokens: bfloat16 [8, 2048, 1024], P('dp', 'seq'), may hold values from -6 to 6
- norm_gains: bfloat16 [2, 1024], P(None, ('dp', 'seq')), may hold values from 0.5 to 1.5
- norm_biases: bfloat16 [2, 1024], P(None, ('dp', 'seq')), may hold values from -1.5 to 1.5
- w_qkv: bfloat16 [1024, 3072], P(('dp', 'seq')), may hold values from -0.1875 to 0.1875
- attn_biases: bfloat16 [2, 1024], P(None, ('dp', 'seq')), may hold values from -2.5 to 2.5
- w_out: bfloat16 [1024, 1024], P(('dp', 'seq')), may hold values from -3 to 3
- branch_biases: bfloat16 [2, 1024], P(None, ('dp', 'seq')), may hold values from -1.5 to 1.5
- w_fc: bfloat16 [1024, 4096], P(('dp', 'seq')), may hold values from -0.1875 to 0.1875
- fc_bias: bfloat16 [4096], P(('dp', 'seq')), may hold values from -2.5 to 2.5
- w_proj: bfloat16 [4096, 1024], P(('dp', 'seq')), may hold values from -0.09375 to 0.09375
- cotangent: bfloat16 [8, 2048, 1024], P('dp', 'seq'), may hold values from -6 to 6
Outputs:
- block_out: bfloat16 [8, 2048, 1024], P('dp', 'seq')
- input_grad: bfloat16 [8, 2048, 1024], P('dp', 'seq')
- grad_norm_gains: float32 [2, 1024], P(None, ('dp', 'seq'))
- grad_norm_biases: float32 [2, 1024], P(None, ('dp', 'seq'))
- grad_w_qkv: float32 [1024, 3072], P(('dp', 'seq'))
- grad_attn_biases: float32 [2, 1024], P(None, ('dp', 'seq'))
- grad_w_out: float32 [1024, 1024], P(('dp', 'seq'))
- grad_branch_biases: float32 [2, 1024], P(None, ('dp', 'seq'))
- grad_w_fc: float32 [1024, 4096], P(('dp', 'seq'))
- grad_fc_bias: float32 [4096], P(('dp', 'seq'))
- grad_w_proj: float32 [4096, 1024], P(('dp', 'seq'))
The draws below stay inside these ranges and needn't reach their ends.
All inputs are finite; a program needn't handle non-finite values.
Results may differ from the reference program's by a relative error of at most 0.034.
Values may be sent and summed in bfloat16 or wider, within the bound.
A program may use at most 192 MiB of HBM per device.

```python
import math
import jax
import jax.numpy as jnp
from jax import lax

D = 1024
H = 16
HEAD = 64
FF = 4096
SEQS = 8
LEN = 2048


def shard_levels(own_key, extent, shards, low, largest):
    factor_of = 1.0
    for axis_at, parts in shards:
        draws = jax.random.uniform(jax.random.fold_in(jax.random.fold_in(own_key, 6), axis_at), (parts,), jnp.float32, low / len(shards), largest / len(shards))
        factor_of = factor_of * jnp.repeat(jnp.exp(draws), extent[axis_at] // parts).reshape((-1,) + (1,) * (len(extent) - 1 - axis_at))
    return factor_of


def scatter_about(own_key, dims, spread, bound, shards=(), held_as=jnp.bfloat16):
    gain = shard_levels(own_key, dims, shards, -0.22, 0.18) if shards else 1.0
    entries = jax.random.normal(own_key, dims, jnp.float32) * spread * gain
    return jnp.minimum(jnp.maximum(entries, -bound), bound).astype(held_as)


def setup_inputs(seed: int = 0) -> dict:
    key_list = jax.random.split(jax.random.key(seed), 12)
    return {
        "tokens": scatter_about(key_list[0], (SEQS, LEN, D), 1.0, 6.0, ((0, 8), (1, 16))),
        "norm_gains": jnp.clip(1.0 + 0.1 * jax.random.normal(key_list[1], (2, D), jnp.float32), 0.5, 1.5).astype(jnp.bfloat16),
        "norm_biases": scatter_about(key_list[2], (2, D), 0.3, 1.5, ((1, 128),)),
        "w_qkv": scatter_about(key_list[3], (D, 3 * D), D ** -0.5, 0.1875, ((0, 128),)),
        "attn_biases": scatter_about(key_list[4], (2, D), 0.5, 2.5, ((1, 128),)),
        "w_out": scatter_about(key_list[5], (D, D), (max(D // 256, 4)) ** -0.5, 3.0, ((0, 128),)),
        "branch_biases": scatter_about(key_list[6], (2, D), 0.3, 1.5, ((1, 128),)),
        "w_fc": scatter_about(key_list[7], (D, FF), D ** -0.5, 0.1875, ((0, 128),)),
        "fc_bias": scatter_about(key_list[8], (FF,), 0.5, 2.5, ((0, 128),)),
        "w_proj": scatter_about(key_list[9], (FF, D), FF ** -0.5, 0.09375, ((0, 128),)),
        "cotangent": scatter_about(key_list[10], (SEQS, LEN, D), 1.0, 6.0, ((0, 8), (1, 16))),
    }


epsilon = 1e-05
masked_score = -1e+30

@jax.custom_vjp
def low(v):
    return lax.optimization_barrier(v.astype(jnp.bfloat16)).astype(jnp.float32)

@jax.custom_vjp
def low_back(v):
    return v

def low_keep(v):
    return (low(v), None)

def low_pass(kept, grad):
    return (grad,)

def back_keep(v):
    return (v, None)

def back_low(kept, grad):
    return (low(grad),)
low.defvjp(low_keep, low_pass)
low_back.defvjp(back_keep, back_low)

def layer_norm(inputs, scaling, offset):
    average = lax.optimization_barrier(jnp.mean(inputs, axis=-1, keepdims=True))
    centred = inputs - average
    variance = lax.optimization_barrier(jnp.mean(centred * centred, axis=-1, keepdims=True))
    return centred * lax.rsqrt(variance + epsilon) * scaling + offset

def gelu_tanh(inputs):
    return 0.5 * inputs * (1.0 + jnp.tanh(0.7978845608028654 * (inputs + 0.044715 * inputs * inputs * inputs)))

def matmul(left, right):
    return jnp.dot(left, right, precision=lax.Precision.HIGHEST)

def attend(query, keys, values):
    length = query.shape[0]
    block_len = min(512, length)
    query3 = query.reshape(length, H, HEAD)
    keys3 = keys.reshape(length, H, HEAD)
    values3 = values.reshape(length, H, HEAD)
    score_scale = 1.0 / math.sqrt(HEAD)
    key_pos = jnp.arange(length).astype(jnp.int32)

    def one_block(index):
        start_row = (index * block_len).astype(jnp.int32)
        query_block = lax.dynamic_slice_in_dim(query3, start_row, block_len, 0)
        scores = jnp.einsum('qhe,khe->hqk', query_block, keys3, precision=lax.Precision.HIGHEST) * score_scale
        scores = low_back(scores)
        query_pos = start_row + jnp.arange(block_len).astype(jnp.int32)
        allowed = key_pos[None, :] <= query_pos[:, None]
        scores = jnp.where(allowed[None], scores, masked_score)
        biggest = lax.optimization_barrier(jnp.max(scores, axis=-1, keepdims=True))
        probs = jnp.exp(scores - biggest)
        probs = probs / lax.optimization_barrier(jnp.sum(probs, axis=-1, keepdims=True))
        probs = low(probs)
        result = jnp.einsum('hqk,khe->qhe', probs, values3, precision=lax.Precision.HIGHEST)
        return result.reshape(block_len, H * HEAD)
    blocks = lax.map(jax.checkpoint(one_block), jnp.arange(length // block_len).astype(jnp.int32))
    return blocks.reshape(length, H * HEAD)

def forward(inputs, norm_gains, norm_biases, w_qkv, attn_biases, w_out, branch_biases, w_fc, fc_bias, w_proj):
    model_width = inputs.shape[1]
    hidden1 = low(layer_norm(inputs, norm_gains[0], norm_biases[0]))
    projected = matmul(hidden1, w_qkv)
    query = low(low_back(projected[:, :model_width] + attn_biases[0]))
    keys = low(low_back(projected[:, model_width:2 * model_width]))
    values = low(low_back(projected[:, 2 * model_width:] + attn_biases[1]))
    attended = low(low_back(attend(query, keys, values)))
    branch = low_back(matmul(attended, w_out) + branch_biases[0])
    middle = inputs + branch
    hidden2 = low(layer_norm(middle, norm_gains[1], norm_biases[1]))
    pre = low_back(matmul(hidden2, w_fc) + fc_bias)
    act = low(gelu_tanh(pre))
    return middle + matmul(act, w_proj) + branch_biases[1]

def reference(tokens, norm_gains, norm_biases, w_qkv, attn_biases, w_out, branch_biases, w_fc, fc_bias, w_proj, cotangent):
    weights_f32 = tuple((item.astype(jnp.float32) for item in (norm_gains, norm_biases, w_qkv, attn_biases, w_out, branch_biases, w_fc, fc_bias, w_proj)))

    def advance(totals, paired):
        seq_in, seq_cot = paired
        seq_out, pullback = jax.vjp(forward, seq_in.astype(jnp.float32), *weights_f32)
        gradients = pullback(seq_cot.astype(jnp.float32))
        totals = tuple((old + new for old, new in zip(totals, gradients[1:])))
        return (totals, (seq_out.astype(jnp.bfloat16), gradients[0].astype(jnp.bfloat16)))
    initial = tuple((jnp.zeros_like(item) for item in weights_f32))
    totals, (outputs, input_grads) = lax.scan(advance, initial, (tokens, cotangent))
    return (outputs, input_grads, totals[0], totals[1], totals[2], totals[3], totals[4], totals[5], totals[6], totals[7], totals[8])
```

```python
import functools
import math

import jax
import jax.numpy as jnp
from jax import lax
from jax.experimental import pallas as pl
from jax.experimental.pallas import tpu as pltpu
from jax.sharding import PartitionSpec as P

MESH = pl.DeviceIdType.MESH
BF16 = jnp.bfloat16
F32 = jnp.float32

H = 16
HEAD = 64
D = 1024
FF = 4096
T = 256
LEN = 2048
HALF = D // 2
FFH = FF // 2
EPS = 1e-05
LOW = -1e30
SCALE2 = math.log2(math.e) / math.sqrt(HEAD)

SMALL0 = 3 * HALF
OUT0 = SMALL0 + 128
FC0 = OUT0 + HALF
W4 = FC0 + FFH
GOUT0 = 3 * HALF
GFC0 = GOUT0 + HALF
G4 = GFC0 + FFH

JB = 512
IB = 256

ORDERS = (("x", "y", "z"), ("y", "z", "x"), ("z", "x", "y"))
SIZES = {"x": 4, "y": 4, "z": 4}


def nt(a, b):
    return lax.dot_general(a, b, (((1,), (1,)), ((), ())), preferred_element_type=F32)


def nn(a, b):
    return jnp.dot(a, b, preferred_element_type=F32)


def mod4(v):
    return lax.rem(v + 4, 4)


def dev(co, core):
    x, y, z = co["x"], co["y"], co["z"]
    return (x * 2 + lax.rem(z, 2), y * 4 + lax.div(z, 2) * 2 + core)


def shift(co, axis, d):
    out = dict(co)
    out[axis] = mod4(co[axis] + d)
    return out


def blocks(ref, sel, c0, n):
    s = slice(None)
    x, y, z = sel["x"], sel["y"], sel["z"]
    return ref.at[
        s if x is None else x,
        s if z is None else lax.rem(z, 2),
        s if y is None else y,
        s if z is None else lax.div(z, 2),
        :,
        pl.ds(c0, n),
    ]


def lead_dims(fixed):
    out = []
    if "x" not in fixed:
        out.append(4)
    if "z" not in fixed:
        out.append(2)
    if "y" not in fixed:
        out.append(4)
    if "z" not in fixed:
        out.append(2)
    return tuple(out)


def half_split(n):
    first = ((n // 128) + 1) // 2 * 128
    return ((0, first), (first, n - first))


def way(d):
    return 0 if d > 0 else 1


class Piece:
    def __init__(self, me, core, ref, c0, n, rot, ssem, rsem, base):
        self.me, self.core, self.ref, self.c0, self.n = me, core, ref, c0, n
        self.order = ORDERS[rot]
        self.ssem, self.rsem, self.base = ssem, rsem, base

    def cols(self, h):
        if h is None:
            return self.c0, self.n
        off, n = half_split(self.n)[h]
        return self.c0 + off, n

    def remote(self, src, dst, ph, st, d):
        i = self.base + ph * 4 + st * 2 + way(d)
        return pltpu.make_async_remote_copy(
            src_ref=src,
            dst_ref=dst,
            send_sem=self.ssem.at[i],
            recv_sem=self.rsem.at[i],
            device_id=dev(shift(self.me, self.order[ph], d), self.core),
            device_id_type=MESH,
        )

    def ways(self, st):
        return (1, -1)


class Gather(Piece):
    def region(self, ph, off, h):
        sel = {}
        for k, a in enumerate(self.order):
            sel[a] = None if k < ph else (mod4(self.me[a] + off) if k == ph else self.me[a])
        return blocks(self.ref, sel, *self.cols(h))

    def copy(self, ph, st, d):
        r = self.region(ph, 0, None) if st == 0 else self.region(ph, -d, way(d))
        return self.remote(r, r, ph, st, d)

    def start(self, ph):
        for d in (1, -1):
            self.copy(ph, 0, d).start()

    def forward(self, ph):
        for d in (1, -1):
            r = self.region(ph, -d, None)
            self.remote(r, r, ph, 0, d).wait_recv()
            self.copy(ph, 1, d).start()

    def finish(self, ph):
        for d in (1, -1):
            r = self.region(ph, -2 * d, way(d))
            self.remote(r, r, ph, 1, d).wait_recv()

    def drain(self):
        for ph in range(3):
            for st in range(2):
                for d in (1, -1):
                    self.copy(ph, st, d).wait_send()


class Reduce(Piece):
    def attach(self, stage):
        self.stage = stage
        return self

    @staticmethod
    def stage_shapes(rows, n, rot, dtype):
        out = []
        (_, n0), (_, n1) = half_split(n)
        for ph in range(3):
            lead = lead_dims(ORDERS[rot][: ph + 1])
            out.append(pltpu.VMEM(lead + (rows, n0), dtype))
            out.append(pltpu.VMEM(lead + (rows, max(n1, 128)), dtype))
            out.append(pltpu.VMEM((2,) + lead + (rows, n), dtype))
        return out

    def region(self, ph, off, h):
        sel = {}
        for k, a in enumerate(self.order):
            sel[a] = self.me[a] if k < ph else (mod4(self.me[a] + off) if k == ph else None)
        return blocks(self.ref, sel, *self.cols(h))

    def ways0(self):
        return (1, -1) if self.n > 128 else (1,)

    def copy(self, ph, st, d):
        if st == 0:
            return self.remote(self.region(ph, 2, way(d)), self.stage[3 * ph + way(d)], ph, 0, d)
        return self.remote(self.region(ph, d, None), self.stage[3 * ph + 2].at[way(d)], ph, 1, d)

    def start(self, ph):
        for d in self.ways0():
            self.copy(ph, 0, d).start()

    def add(self, target, sources, lead):
        def one(idx):
            total = target[idx].astype(F32)
            for s in sources:
                total = total + s[idx].astype(F32)
            target[idx] = total.astype(target.dtype)

        if not lead:
            one(Ellipsis)
        else:
            lax.fori_loop(0, lead[0], lambda i, c: (one(i), c)[1], 0)

    def forward(self, ph):
        lead = lead_dims(self.order[: ph + 1])
        for d in (1, -1):
            if d in self.ways0():
                self.copy(ph, 0, d).wait_recv()
                self.add(self.region(ph, d, way(d)), [self.stage[3 * ph + way(d)]], lead)
            self.copy(ph, 1, d).start()

    def finish(self, ph, out=None):
        lead = lead_dims(self.order[: ph + 1])
        s = self.stage[3 * ph + 2]
        for d in (1, -1):
            self.copy(ph, 1, d).wait_recv()
        mine = self.region(ph, 0, None)
        if out is None:
            self.add(mine, [s.at[0], s.at[1]], lead)
        else:
            out[...] = mine[...].astype(F32) + s[0].astype(F32) + s[1].astype(F32)

    def drain(self):
        for ph in range(3):
            for d in self.ways0():
                self.copy(ph, 0, d).wait_send()
            for d in (1, -1):
                self.copy(ph, 1, d).wait_send()


GATHER_A = (("w4", 0, HALF, 0), ("w4", HALF, HALF, 1), ("w4", 2 * HALF, HALF + 128, 2))
GATHER_B = (
    ("w4", OUT0, HALF + 1024, 0),
    ("w4", FC0 + 1024, 1024, 1),
    ("wp", 768, 256, 1),
    ("wp", 0, 768, 2),
)
REDUCE_F = (
    ("g4", GFC0, 1280, 0),
    ("g4", GFC0 + 1280, 768, 1),
    ("gp", 0, 256, 1),
    ("gp", 256, 768, 2),
)
REDUCE_Q = (("g4", 0, 640, 0), ("g4", 640, 640, 1), ("g4", 1280, 768, 2), ("gs", 0, 128, 0))
ROWS = {"g4": 16, "gp": 32, "gs": 8}
TYPES = {"g4": BF16, "gp": BF16, "gs": F32}


def rows_loop(total, step, body, init=0):
    def one(i, c):
        return body(pl.ds(pl.multiple_of(i * step, step), step), c)

    return lax.fori_loop(0, total // step, one, init)


def fold8(v):
    return jnp.sum(v.reshape(v.shape[0] // 8, 8, v.shape[1]), axis=0)


def norm_stats(v):
    average = jnp.mean(v, axis=-1, keepdims=True)
    centred = v - average
    variance = jnp.mean(centred * centred, axis=-1, keepdims=True)
    inv = lax.rsqrt(variance + EPS)
    return centred * inv, inv


def norm_back(xhat, inv, dh, gain):
    a = dh * gain
    return inv * (
        a - jnp.mean(a, axis=-1, keepdims=True) - xhat * jnp.mean(a * xhat, axis=-1, keepdims=True)
    )


SCRATCH = dict(
    w4=pltpu.VMEM((4, 2, 4, 2, 16, W4), BF16),
    wp=pltpu.VMEM((4, 2, 4, 2, 32, D), BF16),
    g4=pltpu.VMEM((4, 2, 4, 2, 16, G4), BF16),
    gp=pltpu.VMEM((4, 2, 4, 2, 32, D), BF16),
    gs=pltpu.VMEM((4, 2, 4, 2, 8, 128), F32),
    wrecv=pltpu.VMEM((8, W4), F32),
    wor=pltpu.VMEM((2, 2, 4, 2, 16, D), BF16),
    x=pltpu.VMEM((T, D), BF16),
    dy=pltpu.VMEM((T, D), BF16),
    h1=pltpu.VMEM((T, D), BF16),
    h2=pltpu.VMEM((T, D), BF16),
    h2t=pltpu.VMEM((D, T), BF16),
    vec=pltpu.VMEM((8, D), F32),
    fcb=pltpu.VMEM((8, FFH), F32),
    qkvs=pltpu.VMEM((3, 8, HEAD, T), BF16),
    qkvt=pltpu.VMEM((3, HEAD, LEN), BF16),
    qz=pltpu.VMEM((2 * HEAD, LEN), BF16),
    dz=pltpu.VMEM((2 * HEAD, LEN), BF16),
    kv=pltpu.VMEM((LEN, 2 * HEAD), BF16),
    qd=pltpu.VMEM((LEN, 2 * HEAD), BF16),
    sbuf=pltpu.VMEM((LEN, IB), F32),
    ot=pltpu.VMEM((HEAD, LEN), F32),
    ots=pltpu.VMEM((HEAD, LEN), BF16),
    lse=pltpu.VMEM((8, LEN), F32),
    rowdot=pltpu.VMEM((8, LEN), F32),
    attt=pltpu.VMEM((8, HEAD, T), BF16),
    part=pltpu.VMEM((T, D), F32),
    partr=pltpu.VMEM((T, D), F32),
    middle=pltpu.VMEM((T, D), F32),
    outp=pltpu.VMEM((T, D), F32),
    outr=pltpu.VMEM((T // 2, D), F32),
    dh=pltpu.VMEM((T, D), F32),
    dhr=pltpu.VMEM((T, D), F32),
    dbr=pltpu.VMEM((T, D), BF16),
    datt=pltpu.VMEM((8, HEAD, T), BF16),
    dqkvt=pltpu.VMEM((3, HEAD, LEN), BF16),
    dqs=pltpu.VMEM((3, 8, HEAD, T), BF16),
    dh1r=pltpu.VMEM((T // 2, D), F32),
    sv=pltpu.VMEM((8, D), F32),
    sfc=pltpu.VMEM((8, FFH), F32),
    fin=pltpu.VMEM((16, G4), F32),
    fins=pltpu.VMEM((8, 128), F32),
    finr=pltpu.VMEM((8, 128), F32),
    ag_s=pltpu.SemaphoreType.DMA((12 * 7,)),
    ag_r=pltpu.SemaphoreType.DMA((12 * 7,)),
    rs_s=pltpu.SemaphoreType.DMA((12 * 8,)),
    rs_r=pltpu.SemaphoreType.DMA((12 * 8,)),
    a2a_s=pltpu.SemaphoreType.DMA((32,)),
    a2a_r=pltpu.SemaphoreType.DMA((32,)),
    px_s=pltpu.SemaphoreType.DMA((16,)),
    px_r=pltpu.SemaphoreType.DMA((16,)),
    loc=pltpu.SemaphoreType.DMA((8,)),
)


def kernel(wpack, tokens, cot, wproj, o_block, o_in, o_w4, o_wp, o_small, *scratch):
    names = list(SCRATCH)
    r = dict(zip(names, scratch[: len(names)]))
    stages = scratch[len(names) :]
    r["dkv"] = r["sbuf"].at[:, 0 : 2 * HEAD]
    r["dh1"] = r["outp"]
    r["dmid"] = r["part"]
    r["gos"] = r["wor"].at[:, :, :, :, :, 0:HALF]
    r["dqt"] = r["ot"]
    dp, sq = lax.axis_index("dp"), lax.axis_index("seq")
    core = lax.rem(sq, 2)
    me = dict(
        x=lax.div(dp, 2),
        y=lax.div(sq, 4),
        z=lax.rem(lax.div(sq, 2), 2) * 2 + lax.rem(dp, 2),
    )
    j_me = lax.div(sq, 2)
    partner = (dp, sq + 1 - 2 * core)

    peers = [dev(shift(me, a, d), core) for a in "xyz" for d in (1, -1)]
    peers.append(partner)
    for dyy, dzz in ((0, 2), (2, 0), (1, 2), (2, 2), (3, 2)):
        peers.append(dev(shift(shift(me, "y", dyy), "z", dzz), core))
    bar = pltpu.get_barrier_semaphore()
    for t in peers:
        pl.semaphore_signal(bar, inc=1, device_id=t, device_id_type=MESH)
    pl.semaphore_wait(bar, len(peers))

    def pair(src, dst, i):
        return pltpu.make_async_remote_copy(
            src_ref=src,
            dst_ref=dst,
            send_sem=r["px_s"].at[i],
            recv_sem=r["px_r"].at[i],
            device_id=partner,
            device_id_type=MESH,
        )

    mine_rows = pl.ds(pl.multiple_of(core * 128, 128), 128)
    their_rows = pl.ds(pl.multiple_of(128 - core * 128, 128), 128)
    half0 = pl.multiple_of(core * HALF, HALF)
    half1 = pl.multiple_of(HALF - core * HALF, HALF)
    own = (me["x"], lax.rem(me["z"], 2), me["y"], lax.div(me["z"], 2))

    def partner_dev_j(t):
        jj = lax.rem(j_me + t, 8)
        return jj, (dp, jj * 2 + core)

    def a2a(k, t, src, dst, to):
        return pltpu.make_async_remote_copy(
            src_ref=src,
            dst_ref=dst,
            send_sem=r["a2a_s"].at[k * 8 + t],
            recv_sem=r["a2a_r"].at[k * 8 + t],
            device_id=to,
            device_id_type=MESH,
        )

    def tok(jj):
        return pl.ds(pl.multiple_of(jj * T, T), T)

    px_w = pair(wpack.at[1 - core], r["wrecv"], 0)
    px_w.start()
    px_x = pair(tokens, r["x"].at[mine_rows], 1)
    px_x.start()
    px_dy = pair(cot, r["dy"].at[mine_rows], 2)
    px_dy.start()
    lc = [
        pltpu.make_async_copy(tokens, r["x"].at[mine_rows], r["loc"].at[0]),
        pltpu.make_async_copy(cot, r["dy"].at[mine_rows], r["loc"].at[1]),
        pltpu.make_async_copy(wproj, r["wp"].at[own], r["loc"].at[2]),
    ]
    for c in lc:
        c.start()
    px_w.wait_recv()
    mine, theirs = wpack[core], r["wrecv"][...]
    first = jnp.where(core == 0, mine, theirs)
    second = jnp.where(core == 0, theirs, mine)
    r["w4"][own] = jnp.concatenate([first, second], axis=0).astype(BF16)
    lc[2].wait()

    def gathers(table, base):
        out = []
        for i, (name, c0, n, rot) in enumerate(table):
            out.append(Gather(me, core, r[name], c0, n, rot, r["ag_s"], r["ag_r"], (base + i) * 12))
        return out

    ga = gathers(GATHER_A, 0)
    gb = gathers(GATHER_B, len(GATHER_A))
    for ph in range(2):
        for g in ga + gb:
            g.start(ph)
        for g in ga + gb:
            g.forward(ph)
        for g in ga + gb:
            g.finish(ph)
    for g in ga:
        g.start(2)
    for g in ga:
        g.forward(2)
    for g in gb:
        g.start(2)
    lc[0].wait()
    lc[1].wait()
    px_x.wait_recv()
    for g in ga:
        g.finish(2)

    lane = lax.broadcasted_iota(jnp.int32, (8, 128), 1)
    vec_t = [jnp.zeros((8, 128), F32) for _ in range(8)]
    fcb_t = [jnp.zeros((8, 128), F32) for _ in range(16)]
    for p in range(64):
        tile = r["w4"][p // 16, (p // 8) % 2, (p // 2) % 4, p % 2, :, SMALL0 : SMALL0 + 128]
        tile = tile.astype(F32)
        lo, hi = tile[0:8], tile[8:16]
        at = 16 * (p % 8)
        both = jnp.where(lane < 8, lo, 0.0) + pltpu.roll(jnp.where(lane < 8, hi, 0.0), 8, 1)
        vec_t[p // 8] = vec_t[p // 8] + (pltpu.roll(both, at, 1) if at else both)
        fc = jnp.where(core == 0, lo, hi)
        fc = jnp.where((lane >= 32) & (lane < 64), fc, 0.0)
        sh = (32 * (p % 4) - 32) % 128
        fcb_t[p // 4] = fcb_t[p // 4] + (pltpu.roll(fc, sh, 1) if sh else fc)
    for k in range(8):
        r["vec"][:, 128 * k : 128 * k + 128] = vec_t[k]
    for k in range(16):
        r["fcb"][:, 128 * k : 128 * k + 128] = fcb_t[k]

    def vrow(i):
        return r["vec"][i : i + 1, :]

    def ln1(rows, c):
        xhat, _ = norm_stats(r["x"][rows, :].astype(F32))
        r["h1"][rows, :] = (xhat * vrow(0) + vrow(2)).astype(BF16)
        return c

    rows_loop(T, 32, ln1)
    for k in range(3):
        w = r["w4"][:, :, :, :, :, k * HALF : (k + 1) * HALF].reshape(D, HALF)
        v = nn(r["h1"][...], w)
        if k == 0:
            v = v + r["vec"][4:5, pl.ds(half0, HALF)]
        if k == 2:
            v = v + r["vec"][5:6, pl.ds(half0, HALF)]
        r["qkvs"][k] = v.T.astype(BF16).reshape(8, HEAD, T)

    def send_a2a1(start):
        for t in range(1, 8):
            jj, to = partner_dev_j(t)
            c = a2a(0, t, r["qkvs"].at[:, jj], r["qkvt"].at[:, :, tok(j_me)], to)
            c.start() if start else c.wait_send()

    send_a2a1(True)
    r["qkvt"][:, :, tok(j_me)] = r["qkvs"][:, j_me]
    for g in gb:
        g.forward(2)
    for t in range(1, 8):
        jj = lax.rem(j_me + 8 - t, 8)
        a2a(0, t, r["qkvs"].at[:, jj], r["qkvt"].at[:, :, tok(jj)], partner).wait_recv()

    r["qz"][0:HEAD, :] = r["qkvt"][0]
    r["qz"][HEAD:, :] = jnp.zeros((HEAD, LEN), BF16)

    def to_rows(ref, parts):
        def one(i, c):
            cols = pl.ds(pl.multiple_of(i * JB, JB), JB)
            stacked = jnp.concatenate([p(cols) for p in parts], axis=0).astype(F32)
            ref[cols, :] = stacked.T.astype(BF16)
            return c

        lax.fori_loop(0, LEN // JB, one, 0)

    to_rows(r["kv"], [lambda cols: r["qkvt"][1, :, cols], lambda cols: r["qkvt"][2, :, cols]])

    row_i = lax.broadcasted_iota(jnp.int32, (JB, IB), 0)
    col_i = lax.broadcasted_iota(jnp.int32, (JB, IB), 1)

    def jcols(jb):
        return pl.ds(pl.multiple_of(jb * JB, JB), JB)

    def attend(ib, c):
        icols = pl.ds(pl.multiple_of(ib * IB, IB), IB)
        q = r["qz"][:, icols]
        nfull = lax.div(ib * IB, JB)

        def fold_max(s):
            return jnp.max(s.reshape(JB // 8, 8, IB), axis=0)

        def scores(jb, m):
            s = nn(r["kv"][jcols(jb), :], q)
            r["sbuf"][jcols(jb), :] = s
            return jnp.maximum(m, fold_max(s))

        m = lax.fori_loop(0, nfull, scores, jnp.full((8, IB), LOW, F32))
        s = nn(r["kv"][jcols(nfull), :], q)
        s = jnp.where(nfull * JB + row_i <= ib * IB + col_i, s, LOW)
        r["sbuf"][jcols(nfull), :] = s
        m = jnp.max(jnp.maximum(m, fold_max(s)), axis=0, keepdims=True) * SCALE2

        def weigh(jb, state):
            l, o = state
            p = jnp.exp2(r["sbuf"][jcols(jb), :] * SCALE2 - m)
            l = l + fold8(p)
            return l, o + nn(r["qkvt"][2, :, jcols(jb)], p.astype(BF16))

        l, o = lax.fori_loop(
            0, nfull + 1, weigh, (jnp.zeros((8, IB), F32), jnp.zeros((HEAD, IB), F32))
        )
        l = jnp.sum(l, axis=0, keepdims=True)
        o = o / l
        r["ot"][:, icols] = o
        r["ots"][:, icols] = o.astype(BF16)
        r["lse"][:, icols] = jnp.broadcast_to(m + jnp.log2(l), (8, IB))
        return c

    lax.fori_loop(0, LEN // IB, attend, 0)

    def send_a2a2(start):
        for t in range(1, 8):
            jj, to = partner_dev_j(t)
            c = a2a(1, t, r["ots"].at[:, tok(jj)], r["attt"].at[j_me], to)
            c.start() if start else c.wait_send()

    send_a2a2(True)
    r["attt"][j_me] = r["ots"][:, tok(j_me)]

    for g in gb:
        g.finish(2)
    keep = r["w4"].at[pl.ds(2 * core, 2), :, :, :, :, pl.ds(OUT0, HALF)]
    give = r["w4"].at[pl.ds(2 - 2 * core, 2), :, :, :, :, pl.ds(OUT0, HALF)]
    wor_mine = r["wor"].at[:, :, :, :, :, pl.ds(half0, HALF)]
    px_wo = pair(give, wor_mine, 3)
    px_wo.start()
    lc_wo = pltpu.make_async_copy(keep, wor_mine, r["loc"].at[3])
    lc_wo.start()
    for t in range(1, 8):
        jj = lax.rem(j_me + 8 - t, 8)
        a2a(1, t, r["ots"].at[:, tok(jj)], r["attt"].at[jj], partner).wait_recv()
    lc_wo.wait()
    px_wo.wait_recv()

    att = r["attt"][...].reshape(8 * HEAD, T).astype(F32).T.astype(BF16)
    r["part"][...] = nn(att, r["wor"][...].reshape(HALF, D))
    px_p = pair(r["part"], r["partr"], 4)
    px_p.start()
    px_p.wait()

    def ln2(rows, c):
        mid = r["x"][rows, :].astype(F32) + (r["part"][rows, :] + r["partr"][rows, :] + vrow(6))
        r["middle"][rows, :] = mid
        xhat, _ = norm_stats(mid)
        r["h2"][rows, :] = (xhat * vrow(1) + vrow(3)).astype(BF16)
        return c

    rows_loop(T, 32, ln2)
    r["h2t"][...] = r["h2"][...].astype(F32).T.astype(BF16)
    r["outp"][...] = jnp.zeros((T, D), F32)
    r["dh"][...] = jnp.zeros((T, D), F32)
    px_dy.wait_recv()

    def ffn(t, c):
        hi, lo = lax.div(t, 2), lax.rem(t, 2)
        cols = pl.ds(pl.multiple_of(t * 256, 256), 256)
        wf = r["w4"][:, :, :, :, :, pl.ds(pl.multiple_of(FC0 + t * 256, 128), 256)].reshape(D, 256)
        wp = r["wp"][hi, lo].reshape(256, D)
        pre = nn(r["h2"][...], wf) + r["fcb"][0:1, cols]
        d_act = nt(r["dy"][...], wp)
        sq_ = pre * pre
        th = jnp.tanh(0.7978845608028654 * (pre + 0.044715 * sq_ * pre))
        act = 0.5 * pre * (1.0 + th)
        slope = 0.5 * (1.0 + th) + 0.5 * pre * (1.0 - th * th) * (
            0.7978845608028654 * (1.0 + 3.0 * 0.044715 * sq_)
        )
        d_pre = (slope * d_act).astype(BF16)
        r["outp"][...] += nn(act.astype(BF16), wp)
        r["gp"][hi, lo] = (
            nn(act.T.astype(BF16), r["dy"][...]).astype(BF16).reshape(4, 2, 32, D)
        )
        r["g4"][:, :, :, :, :, pl.ds(pl.multiple_of(GFC0 + t * 256, 256), 256)] = (
            nn(r["h2t"][...], d_pre).astype(BF16).reshape(4, 2, 4, 2, 16, 256)
        )
        r["sfc"][:, cols] = jnp.broadcast_to(
            jnp.sum(d_pre.astype(F32), axis=0, keepdims=True), (8, 256)
        )
        r["dh"][...] += nt(d_pre, wf)
        return c

    lax.fori_loop(0, 8, ffn, 0)

    px_dh = pair(r["dh"], r["dhr"], 5)
    px_dh.start()
    px_out = pair(r["outp"].at[their_rows], r["outr"], 6)
    px_out.start()

    def reduces(table, base, stage_at):
        out = []
        for i, (name, c0, n, rot) in enumerate(table):
            piece = Reduce(me, core, r[name], c0, n, rot, r["rs_s"], r["rs_r"], (base + i) * 12)
            k = (stage_at + i) * 9
            out.append(piece.attach(stages[k : k + 9]))
        return out

    rf = reduces(REDUCE_F, 0, 0)
    rq = reduces(REDUCE_Q, len(REDUCE_F), len(REDUCE_F))
    for g in rf:
        g.start(0)

    r["sv"][...] = jnp.zeros((8, D), F32)
    px_dh.wait_recv()

    def ln2_back(rows, c):
        dh = r["dh"][rows, :] + r["dhr"][rows, :]
        r["dhr"][rows, :] = dh
        xhat, inv = norm_stats(r["middle"][rows, :])
        d_mid = r["dy"][rows, :].astype(F32) + norm_back(xhat, inv, dh, vrow(1))
        r["dmid"][rows, :] = d_mid
        r["dbr"][rows, :] = d_mid.astype(BF16)
        return c

    rows_loop(T, 32, ln2_back)

    wor = r["wor"][...].reshape(HALF, D)
    r["datt"][...] = nt(wor, r["dbr"][...]).astype(BF16).reshape(8, HEAD, T)

    def send_a2a3(start):
        for t in range(1, 8):
            jj, to = partner_dev_j(t)
            c = a2a(2, t, r["datt"].at[jj], r["dz"].at[pl.ds(HEAD, HEAD), tok(j_me)], to)
            c.start() if start else c.wait_send()

    send_a2a3(True)
    r["dz"][HEAD:, tok(j_me)] = r["datt"][j_me]
    r["dz"][0:HEAD, :] = jnp.zeros((HEAD, LEN), BF16)

    gout = nn(r["attt"][...].reshape(HALF, T), r["dbr"][...]).astype(BF16)
    left = gout[:, :HALF].reshape(2, 2, 4, 2, 16, HALF)
    right = gout[:, HALF:].reshape(2, 2, 4, 2, 16, HALF)
    go_at = r["g4"].at[pl.ds(2 * core, 2), :, :, :, :, pl.ds(GOUT0, HALF)]
    go_at[...] = jnp.where(core == 0, left, right)
    r["gos"][...] = jnp.where(core == 0, right, left)
    px_go = pair(r["gos"], go_at, 7)
    px_go.start()

    def small2(i, c):
        s1, s2, s3, s4 = c
        rows = pl.ds(pl.multiple_of(core * 128 + i * 32, 32), 32)
        dh = r["dhr"][rows, :]
        xhat, _ = norm_stats(r["middle"][rows, :])
        return (
            s1 + fold8(dh * xhat),
            s2 + fold8(dh),
            s3 + fold8(r["dbr"][rows, :].astype(F32)),
            s4 + fold8(r["dy"][rows, :].astype(F32)),
        )

    zero = jnp.zeros((8, D), F32)
    sums = lax.fori_loop(0, 4, small2, (zero, zero, zero, zero))
    for row, s in zip((1, 3, 6, 7), sums):
        r["sv"][row : row + 1, :] = jnp.sum(s, axis=0, keepdims=True)

    px_out.wait_recv()

    def block_out(i, c):
        rows = pl.ds(pl.multiple_of(core * 128 + i * 32, 32), 32)
        here = pl.ds(pl.multiple_of(i * 32, 32), 32)
        o_block[here, :] = (
            r["middle"][rows, :] + (r["outp"][rows, :] + r["outr"][here, :]) + vrow(7)
        ).astype(BF16)
        return c

    lax.fori_loop(0, 4, block_out, 0)
    px_out.wait_send()

    for g in rf:
        g.forward(0)

    for t in range(1, 8):
        jj = lax.rem(j_me + 8 - t, 8)
        a2a(2, t, r["datt"].at[jj], r["dz"].at[pl.ds(HEAD, HEAD), tok(jj)], partner).wait_recv()

    to_rows(r["qd"], [lambda cols: r["qz"][0:HEAD, cols], lambda cols: r["dz"][HEAD:, cols]])
    r["rowdot"][...] = jnp.broadcast_to(
        jnp.sum(r["dz"][HEAD:, :].astype(F32) * r["ot"][...], axis=0, keepdims=True), (8, LEN)
    )
    r["dkv"][...] = jnp.zeros((LEN, 2 * HEAD), F32)
    lane_kv = lax.broadcasted_iota(jnp.int32, (JB, 2 * HEAD), 1)

    def attend_back(ib, c):
        icols = pl.ds(pl.multiple_of(ib * IB, IB), IB)
        q, do = r["qz"][:, icols], r["dz"][:, icols]
        qd = r["qd"][icols, :]
        lse, dot = r["lse"][0:1, icols], r["rowdot"][0:1, icols]
        nfull = lax.div(ib * IB, JB)

        def step(jb, dq, masked):
            kv = r["kv"][jcols(jb), :]
            p = jnp.exp2(nn(kv, q) * SCALE2 - lse)
            if masked:
                p = jnp.where(jb * JB + row_i <= ib * IB + col_i, p, 0.0)
            ds = (p * (nn(kv, do) - dot)).astype(BF16)
            r["dkv"][jcols(jb), :] += jnp.where(
                lane_kv < HEAD, nn(ds, qd), nn(p.astype(BF16), qd)
            )
            return dq + nn(r["qkvt"][1, :, jcols(jb)], ds)

        dq = lax.fori_loop(
            0, nfull, lambda jb, a: step(jb, a, False), jnp.zeros((HEAD, IB), F32)
        )
        r["dqt"][:, icols] = step(nfull, dq, True)

        @pl.when(ib == 3)
        def _():
            for g in rf:
                g.finish(0)
            for g in rf:
                g.start(1)

        @pl.when(ib == 5)
        def _():
            for g in rf:
                g.forward(1)

        return c

    lax.fori_loop(0, LEN // IB, attend_back, 0)

    r["dqkvt"][0] = (r["dqt"][...] * 0.125).astype(BF16)

    def kv_back(jb, c):
        both = r["dkv"][jcols(jb), :].T
        r["dqkvt"][1, :, jcols(jb)] = (both[:HEAD] * 0.125).astype(BF16)
        r["dqkvt"][2, :, jcols(jb)] = both[HEAD:].astype(BF16)
        return c

    lax.fori_loop(0, LEN // JB, kv_back, 0)

    def send_a2a4(start):
        for t in range(1, 8):
            jj, to = partner_dev_j(t)
            c = a2a(3, t, r["dqkvt"].at[:, :, tok(jj)], r["dqs"].at[:, j_me], to)
            c.start() if start else c.wait_send()

    send_a2a4(True)
    r["dqs"][:, j_me] = r["dqkvt"][:, :, tok(j_me)]
    for g in rf:
        g.finish(1)
    for g in rf:
        g.start(2)
    for t in range(1, 8):
        jj = lax.rem(j_me + 8 - t, 8)
        a2a(3, t, r["dqkvt"].at[:, :, tok(jj)], r["dqs"].at[:, jj], partner).wait_recv()

    h1t = r["h1"][...].astype(F32).T.astype(BF16)
    for k in range(3):
        dt = r["dqs"][k].reshape(HALF, T)
        r["g4"][:, :, :, :, :, k * HALF : (k + 1) * HALF] = (
            nt(h1t, dt).astype(BF16).reshape(4, 2, 4, 2, 16, HALF)
        )
    px_go.wait_recv()
    for g in rq[:3]:
        g.start(0)
    for k in range(3):
        d = r["dqs"][k].reshape(HALF, T).astype(F32).T
        if k != 1:
            row = 4 if k == 0 else 5
            r["sv"][row : row + 1, pl.ds(half0, HALF)] = jnp.sum(d, axis=0, keepdims=True)
        w = r["w4"][:, :, :, :, :, k * HALF : (k + 1) * HALF].reshape(D, HALF)
        v = nt(d.astype(BF16), w)
        r["dh1"][...] = v if k == 0 else r["dh1"][...] + v
    px_d1 = pair(r["dh1"].at[their_rows], r["dh1r"], 8)
    px_d1.start()
    for g in rf:
        g.forward(2)
    px_d1.wait_recv()

    def ln1_back(i, c):
        s1, s2 = c
        rows = pl.ds(pl.multiple_of(core * 128 + i * 32, 32), 32)
        here = pl.ds(pl.multiple_of(i * 32, 32), 32)
        dh = r["dh1"][rows, :] + r["dh1r"][here, :]
        xhat, inv = norm_stats(r["x"][rows, :].astype(F32))
        d_in = r["dmid"][rows, :] + norm_back(xhat, inv, dh, vrow(0))
        o_in[here, :] = d_in.astype(BF16)
        return s1 + fold8(dh * xhat), s2 + fold8(dh)

    sums = lax.fori_loop(0, 4, ln1_back, (zero, zero))
    for row, s in zip((0, 2), sums):
        r["sv"][row : row + 1, :] = jnp.sum(s, axis=0, keepdims=True)

    for p in range(64):
        k, at = p // 8, 16 * (p % 8)
        v = r["sv"][:, 128 * k : 128 * k + 128]
        v = pltpu.roll(v, (128 - at) % 128, 1) if at else v
        k, sh = p // 4, (32 - 32 * (p % 4)) % 128
        f = r["sfc"][:, 128 * k : 128 * k + 128]
        f = pltpu.roll(f, sh, 1) if sh else f
        r["gs"][p // 16, (p // 8) % 2, (p // 2) % 4, p % 2] = jnp.where(
            lane < 16, v, jnp.where((lane >= 32) & (lane < 64), f, 0.0)
        )
    rq[3].start(0)

    def out_of(g, wide, tall):
        return wide.at[:, pl.ds(g.c0, g.n)] if tall is None else tall.at[:, pl.ds(g.c0, g.n)]

    for ph in range(3):
        for g in rq:
            g.forward(ph)
        if ph == 0:
            for g in rf:
                g.finish(2, out_of(g, r["fin"], o_wp if g.ref is r["gp"] else None))
        for i, g in enumerate(rq):
            out = None
            if ph == 2:
                out = r["fins"] if i == 3 else out_of(g, r["fin"], None)
            g.finish(ph, out)
            if ph < 2:
                g.start(ph + 1)

    mine8 = pl.ds(pl.multiple_of(core * 8, 8), 8)
    their8 = pl.ds(pl.multiple_of(8 - core * 8, 8), 8)
    px_f = pair(r["fin"].at[their8], o_w4.at[core], 9)
    px_f.start()
    px_s = pair(r["fins"], r["finr"], 10)
    px_s.start()
    o_w4[core] = r["fin"][mine8, :]
    px_f.wait_recv()
    px_s.wait_recv()
    total = r["fins"][...] + jnp.where(lane < 16, r["finr"][...], 0.0)
    shifted = jnp.where(core == 0, total, pltpu.roll(total, 120, 1))
    o_small[...] = jnp.where(lane < 8, shifted, total)

    for g in ga + gb + rf + rq:
        g.drain()
    for c in (px_w, px_x, px_dy, px_wo, px_dh, px_go, px_d1, px_f, px_s):
        c.wait_send()
    send_a2a1(False)
    send_a2a2(False)
    send_a2a3(False)
    send_a2a4(False)


def stage_list():
    out = []
    for name, _, n, rot in REDUCE_F + REDUCE_Q:
        out += Reduce.stage_shapes(ROWS[name], n, rot, TYPES[name])
    return out


def block(wpack, tokens, cot, wproj):
    vm = pl.BlockSpec(memory_space=pltpu.VMEM)
    return pl.pallas_call(
        kernel,
        out_shape=(
            jax.ShapeDtypeStruct((128, D), BF16),
            jax.ShapeDtypeStruct((128, D), BF16),
            jax.ShapeDtypeStruct((2, 8, G4), F32),
            jax.ShapeDtypeStruct((32, D), F32),
            jax.ShapeDtypeStruct((8, 128), F32),
        ),
        in_specs=[vm] * 4,
        out_specs=(vm,) * 5,
        scratch_shapes=list(SCRATCH.values()) + stage_list(),
        compiler_params=pltpu.CompilerParams(
            collective_id=0, has_side_effects=True, vmem_limit_bytes=63 * 2**20
        ),
    )(wpack, tokens, cot, wproj)


def on_device(
    tokens,
    norm_gains,
    norm_biases,
    w_qkv,
    attn_biases,
    w_out,
    branch_biases,
    w_fc,
    fc_bias,
    w_proj,
    cotangent,
):
    q = w_qkv.reshape(8, 3, 2, HALF).transpose(2, 0, 1, 3).reshape(2, 8, 3 * HALF)
    o = w_out.reshape(8, 2, HALF).transpose(1, 0, 2)
    f = w_fc.reshape(8, 64, 2, 32).transpose(2, 0, 1, 3).reshape(2, 8, FFH)
    vectors = jnp.concatenate([norm_gains, norm_biases, attn_biases, branch_biases], axis=0)
    fcb = jnp.concatenate([fc_bias[None], jnp.zeros((7, 32), BF16)], axis=0)
    small = jnp.concatenate(
        [vectors, jnp.zeros((8, 24), BF16), fcb, jnp.zeros((8, 64), BF16)], axis=1
    )
    small = jnp.broadcast_to(small[None], (2, 8, 128))
    wpack = jnp.concatenate([q, small, o, f], axis=2).astype(F32)
    block_out, input_grad, gw4, gwp, gsmall = block(wpack, tokens[0], cotangent[0], w_proj)
    gq = gw4[:, :, :GOUT0].reshape(2, 8, 3, HALF).transpose(1, 2, 0, 3).reshape(8, 3 * D)
    go = gw4[:, :, GOUT0:GFC0].transpose(1, 0, 2).reshape(8, D)
    gf = gw4[:, :, GFC0:].reshape(2, 8, 64, 32).transpose(1, 2, 0, 3).reshape(8, FF)
    return (
        block_out[None],
        input_grad[None],
        gsmall[0:2, :8],
        gsmall[2:4, :8],
        gq,
        gsmall[4:6, :8],
        go,
        gsmall[6:8, :8],
        gf,
        gsmall[0, 32:64],
        gwp,
    )


def solution(mesh):
    in_specs = (
        P("dp", "seq", None),
        P(None, ("dp", "seq")),
        P(None, ("dp", "seq")),
        P(("dp", "seq"), None),
        P(None, ("dp", "seq")),
        P(("dp", "seq"), None),
        P(None, ("dp", "seq")),
        P(("dp", "seq"), None),
        P(("dp", "seq")),
        P(("dp", "seq"), None),
        P("dp", "seq", None),
    )
    out_specs = (
        P("dp", "seq", None),
        P("dp", "seq", None),
        P(None, ("dp", "seq")),
        P(None, ("dp", "seq")),
        P(("dp", "seq"), None),
        P(None, ("dp", "seq")),
        P(("dp", "seq"), None),
        P(None, ("dp", "seq")),
        P(("dp", "seq"), None),
        P(("dp", "seq")),
        P(("dp", "seq"), None),
    )
    return jax.shard_map(
        on_device, mesh=mesh, in_specs=in_specs, out_specs=out_specs, check_vma=False
    )
```

```python
import functools
import math

import jax
import jax.numpy as jnp
from jax import lax
from jax.experimental import pallas as pl
from jax.experimental.pallas import tpu as pltpu
from jax.sharding import PartitionSpec as P

MESH = pl.DeviceIdType.MESH
BF16 = jnp.bfloat16
F32 = jnp.float32

H = 16
HEAD = 64
D = 1024
FF = 4096
T = 256
LEN = 2048
HALF = D // 2
FFH = FF // 2
EPS = 1e-05
LOW = -1e30
SCALE2 = math.log2(math.e) / math.sqrt(HEAD)

SMALL0 = 3 * HALF
OUT0 = SMALL0 + 128
FC0 = OUT0 + HALF
W4 = FC0 + FFH
GOUT0 = 0
GFC0 = HALF
G4 = GFC0 + FFH

JB = 512
IB = 256

ORDERS = (("x", "y", "z"), ("y", "z", "x"), ("z", "x", "y"))
SIZES = {"x": 4, "y": 4, "z": 4}


def nt(a, b):
    return lax.dot_general(a, b, (((1,), (1,)), ((), ())), preferred_element_type=F32)


def nn(a, b):
    return jnp.dot(a, b, preferred_element_type=F32)


def mod4(v):
    return lax.rem(v + 4, 4)


def dev(co, core):
    x, y, z = co["x"], co["y"], co["z"]
    return (x * 2 + lax.rem(z, 2), y * 4 + lax.div(z, 2) * 2 + core)


def shift(co, axis, d):
    out = dict(co)
    out[axis] = mod4(co[axis] + d)
    return out


def blocks(ref, sel, c0, n):
    s = slice(None)
    x, y, z = sel["x"], sel["y"], sel["z"]
    return ref.at[
        s if x is None else x,
        s if z is None else lax.rem(z, 2),
        s if y is None else y,
        s if z is None else lax.div(z, 2),
        :,
        pl.ds(c0, n),
    ]


def lead_dims(fixed):
    out = []
    if "x" not in fixed:
        out.append(4)
    if "z" not in fixed:
        out.append(2)
    if "y" not in fixed:
        out.append(4)
    if "z" not in fixed:
        out.append(2)
    return tuple(out)


def half_split(n):
    first = ((n // 128) + 1) // 2 * 128
    return ((0, first), (first, n - first))


def way(d):
    return 0 if d > 0 else 1


def remote_copy(src, dst, sems, i, to):
    return pltpu.make_async_remote_copy(
        src_ref=src,
        dst_ref=dst,
        send_sem=sems[0].at[i],
        recv_sem=sems[1].at[i],
        device_id=to,
        device_id_type=MESH,
    )


ring_copy = remote_copy


class Piece:
    def __init__(self, me, core, ref, c0, n, rot, sems, base):
        self.me, self.core, self.ref, self.c0, self.n = me, core, ref, c0, n
        self.order = ORDERS[rot]
        self.sems, self.base = sems, base

    def cols(self, h):
        if h is None:
            return self.c0, self.n
        off, n = half_split(self.n)[h]
        return self.c0 + off, n

    def remote(self, src, dst, ph, st, d):
        to = dev(shift(self.me, self.order[ph], d), self.core)
        return ring_copy(src, dst, self.sems, self.base + ph * 4 + st * 2 + way(d), to)


class Gather(Piece):
    def region(self, ph, off, h):
        sel = {}
        for k, a in enumerate(self.order):
            sel[a] = None if k < ph else (mod4(self.me[a] + off) if k == ph else self.me[a])
        return blocks(self.ref, sel, *self.cols(h))

    def ways1(self):
        return (1, -1) if self.n > 128 else (1,)

    def copy(self, ph, st, d):
        r = self.region(ph, 0, None) if st == 0 else self.region(ph, -d, way(d))
        return self.remote(r, r, ph, st, d)

    def start(self, ph):
        for d in (1, -1):
            self.copy(ph, 0, d).start()

    def forward(self, ph):
        for d in (1, -1):
            r = self.region(ph, -d, None)
            self.remote(r, r, ph, 0, d).wait_recv()
            if d in self.ways1():
                self.copy(ph, 1, d).start()

    def finish(self, ph):
        for d in self.ways1():
            r = self.region(ph, -2 * d, way(d))
            self.remote(r, r, ph, 1, d).wait_recv()

    def drain(self):
        for ph in range(3):
            for d in (1, -1):
                self.copy(ph, 0, d).wait_send()
            for d in self.ways1():
                self.copy(ph, 1, d).wait_send()


class Reduce(Piece):
    def attach(self, stage):
        self.stage = stage
        return self

    @staticmethod
    def stage_shapes(rows, n, rot, dtype):
        out = []
        (_, n0), (_, n1) = half_split(n)
        for ph in range(3):
            lead = lead_dims(ORDERS[rot][: ph + 1])
            out.append(pltpu.VMEM(lead + (rows, n0), dtype))
            out.append(pltpu.VMEM(lead + (rows, max(n1, 128)), dtype))
            out.append(pltpu.VMEM((2,) + lead + (rows, n), dtype))
        return out

    def region(self, ph, off, h):
        sel = {}
        for k, a in enumerate(self.order):
            sel[a] = self.me[a] if k < ph else (mod4(self.me[a] + off) if k == ph else None)
        return blocks(self.ref, sel, *self.cols(h))

    def ways0(self):
        return (1, -1) if self.n > 128 else (1,)

    def copy(self, ph, st, d):
        if st == 0:
            return self.remote(self.region(ph, 2, way(d)), self.stage[3 * ph + way(d)], ph, 0, d)
        return self.remote(self.region(ph, d, None), self.stage[3 * ph + 2].at[way(d)], ph, 1, d)

    def start(self, ph):
        for d in self.ways0():
            self.copy(ph, 0, d).start()

    def add(self, target, sources, lead):
        def one(idx):
            total = target[idx]
            for s in sources:
                total = total + s[idx]
            target[idx] = total

        if not lead:
            one(Ellipsis)
        else:
            lax.fori_loop(0, lead[0], lambda i, c: (one(i), c)[1], 0)

    def forward(self, ph):
        lead = lead_dims(self.order[: ph + 1])
        for d in (1, -1):
            if d in self.ways0():
                self.copy(ph, 0, d).wait_recv()
                self.add(self.region(ph, d, way(d)), [self.stage[3 * ph + way(d)]], lead)
            self.copy(ph, 1, d).start()

    def finish(self, ph, out=None):
        lead = lead_dims(self.order[: ph + 1])
        s = self.stage[3 * ph + 2]
        for d in (1, -1):
            self.copy(ph, 1, d).wait_recv()
        mine = self.region(ph, 0, None)
        if out is None:
            self.add(mine, [s.at[0], s.at[1]], lead)
        else:
            out[...] = mine[...].astype(F32) + s[0].astype(F32) + s[1].astype(F32)

    def drain(self):
        for ph in range(3):
            for d in self.ways0():
                self.copy(ph, 0, d).wait_send()
            for d in (1, -1):
                self.copy(ph, 1, d).wait_send()


GATHER_B = (
    ("w4", OUT0, HALF + 256, 0),
    ("w4", FC0 + 256, 768, 1),
    ("w4", FC0 + 1024, 768, 2),
)
GATHER_C = (
    ("w4", FC0 + 1792, 256, 0),
    ("wp", 0, 256, 0),
    ("wp", 256, 384, 1),
    ("wp", 640, 384, 2),
)
GATHER_A = (("w4", 0, HALF, 0), ("w4", HALF, HALF, 1), ("w4", 2 * HALF, HALF + 128, 2))
REDUCE_P = (("gp", 0, HALF, 1), ("gp", HALF, HALF, 2))
REDUCE_F = (
    ("g4", GFC0, 640, 0),
    ("g4", GFC0 + 640, 640, 0),
    ("g4", GFC0 + 1280, 256, 1),
    ("g4", GFC0 + 1536, HALF, 2),
)
REDUCE_O = (("g4", GOUT0, HALF, 0),)
ROWS = {"g4": 16, "gp": 32}


def rows_loop(total, step, body, init=0):
    def one(i, c):
        return body(pl.ds(pl.multiple_of(i * step, step), step), c)

    return lax.fori_loop(0, total // step, one, init)


def fold8(v):
    return jnp.sum(v.reshape(v.shape[0] // 8, 8, v.shape[1]), axis=0)


def norm_stats(v):
    average = jnp.mean(v, axis=-1, keepdims=True)
    centred = v - average
    variance = jnp.mean(centred * centred, axis=-1, keepdims=True)
    inv = lax.rsqrt(variance + EPS)
    return centred * inv, inv


def norm_back(xhat, inv, dh, gain):
    a = dh * gain
    return inv * (
        a - jnp.mean(a, axis=-1, keepdims=True) - xhat * jnp.mean(a * xhat, axis=-1, keepdims=True)
    )


SCRATCH = dict(
    w4=pltpu.VMEM((4, 2, 4, 2, 16, W4), BF16),
    wp=pltpu.VMEM((4, 2, 4, 2, 32, D), BF16),
    g4=pltpu.VMEM((4, 2, 4, 2, 16, G4), BF16),
    gp=pltpu.VMEM((4, 2, 4, 2, 32, D), BF16),
    pack=pltpu.VMEM((2, 8, W4), F32),
    tiny=pltpu.VMEM((2, 8, 128), F32),
    wrecv=pltpu.VMEM((8, W4), F32),
    wor=pltpu.VMEM((2, 2, 4, 2, 16, D), BF16),
    hs=pltpu.VMEM((4, 2, 2, 128, D), BF16),
    h1=pltpu.VMEM((T, D), BF16),
    qkvs=pltpu.VMEM((3, 8, HEAD, T), BF16),
    qkvt=pltpu.VMEM((3, HEAD, LEN), BF16),
    x=pltpu.VMEM((T, D), BF16),
    dy=pltpu.VMEM((T, D), BF16),
    h2=pltpu.VMEM((T, D), BF16),
    h2t=pltpu.VMEM((D, T), BF16),
    vec=pltpu.VMEM((8, D), F32),
    fcb=pltpu.VMEM((8, FFH), F32),
    qz=pltpu.VMEM((2 * HEAD, LEN), BF16),
    dz=pltpu.VMEM((2 * HEAD, LEN), BF16),
    kv=pltpu.VMEM((LEN, 2 * HEAD), BF16),
    qd=pltpu.VMEM((LEN, 2 * HEAD), BF16),
    sbuf=pltpu.VMEM((LEN, IB), F32),
    ot=pltpu.VMEM((HEAD, LEN), F32),
    ots=pltpu.VMEM((HEAD, LEN), BF16),
    lse=pltpu.VMEM((8, LEN), F32),
    rowdot=pltpu.VMEM((8, LEN), F32),
    attt=pltpu.VMEM((8, HEAD, T), BF16),
    act=pltpu.VMEM((T, FFH), BF16),
    dpre=pltpu.VMEM((T, FFH), BF16),
    part=pltpu.VMEM((T, D), F32),
    partr=pltpu.VMEM((T, D), F32),
    middle=pltpu.VMEM((T, D), F32),
    outp=pltpu.VMEM((T, D), F32),
    outr=pltpu.VMEM((T // 2, D), F32),
    dh=pltpu.VMEM((T, D), F32),
    dhr=pltpu.VMEM((T, D), F32),
    dbr=pltpu.VMEM((T, D), BF16),
    datt=pltpu.VMEM((8, HEAD, T), BF16),
    dqkvt=pltpu.VMEM((3, HEAD, LEN), BF16),
    dqs=pltpu.VMEM((3, 8, HEAD, T), BF16),
    dh1r=pltpu.VMEM((T // 2, D), F32),
    gqs=pltpu.VMEM((8, 3 * HEAD, 128), BF16),
    gqr=pltpu.VMEM((8, 3 * HEAD, 128), BF16),
    gqt=pltpu.VMEM((8, 16, 256), F32),
    finq=pltpu.VMEM((8, 16, 256), F32),
    sv=pltpu.VMEM((8, D), F32),
    sfc=pltpu.VMEM((8, FFH), F32),
    ss=pltpu.VMEM((8, 16, 128), F32),
    ssr=pltpu.VMEM((8, 16, 128), F32),
    st=pltpu.VMEM((16, 128), F32),
    str=pltpu.VMEM((8, 16, 128), F32),
    fin=pltpu.VMEM((16, G4), F32),
    fins=pltpu.VMEM((16, 128), F32),
    finr=pltpu.VMEM((16, 128), F32),
    ag_s=pltpu.SemaphoreType.DMA((12 * 10,)),
    ag_r=pltpu.SemaphoreType.DMA((12 * 10,)),
    rs_s=pltpu.SemaphoreType.DMA((12 * 7,)),
    rs_r=pltpu.SemaphoreType.DMA((12 * 7,)),
    xg_s=pltpu.SemaphoreType.DMA((6,)),
    xg_r=pltpu.SemaphoreType.DMA((6,)),
    a2a_s=pltpu.SemaphoreType.DMA((48,)),
    a2a_r=pltpu.SemaphoreType.DMA((48,)),
    dp_s=pltpu.SemaphoreType.DMA((24,)),
    dp_r=pltpu.SemaphoreType.DMA((24,)),
    px_s=pltpu.SemaphoreType.DMA((16,)),
    px_r=pltpu.SemaphoreType.DMA((16,)),
    loc=pltpu.SemaphoreType.DMA((8,)),
)


def roll(v, shift):
    shift %= 128
    return pltpu.roll(v, shift, 1) if shift else v


def quarters(pieces):
    lane = lax.broadcasted_iota(jnp.int32, (8, 128), 1)
    low = jnp.where(lane < 32, pieces[0], pieces[1])
    high = jnp.where(lane < 96, pieces[2], pieces[3])
    return jnp.where(lane < 64, low, high)


def pack(pack_ref, tiny, w_qkv, w_out, w_fc, vectors, fc_bias):
    q, o, f = w_qkv[...].astype(F32), w_out[...].astype(F32), w_fc[...].astype(F32)
    lane = lax.broadcasted_iota(jnp.int32, (8, 128), 1)
    tiny[...] = jnp.zeros((2, 8, 128), F32)
    for i, v in enumerate(vectors):
        tiny[0, 2 * i : 2 * i + 2, 0:8] = v[...].astype(F32)
    tiny[1, 0:1, 0:32] = fc_bias[...].astype(F32)
    small = jnp.where(lane < 8, tiny[0], roll(tiny[1], 32))
    for h in range(2):
        for k in range(3):
            c = k * D + h * HALF
            pack_ref[h, :, k * HALF : (k + 1) * HALF] = q[:, c : c + HALF]
        pack_ref[h, :, SMALL0 : SMALL0 + 128] = small
        pack_ref[h, :, OUT0 : OUT0 + HALF] = o[:, h * HALF : (h + 1) * HALF]
        for m in range(16):
            first = f[:, 256 * m : 256 * m + 128]
            second = f[:, 256 * m + 128 : 256 * m + 256]
            pack_ref[h, :, FC0 + 128 * m : FC0 + 128 * m + 128] = quarters(
                [
                    roll(first, -32 * h),
                    roll(first, -32 - 32 * h),
                    roll(second, 64 - 32 * h),
                    roll(second, 32 - 32 * h),
                ]
            )


def unpack(block, grad_in, w4, wq, wp, small, *outs):
    o_block, o_in, o_gains, o_shifts, o_qkv, o_attn, o_out, o_branch, o_fc, o_fcb, o_proj = outs
    o_block[...] = block[...]
    o_in[...] = grad_in[...]
    o_proj[...] = wp[...]
    for i, o in enumerate((o_gains, o_shifts, o_attn, o_branch)):
        o[...] = small[2 * i : 2 * i + 2, 0:8]
    o_fcb[...] = roll(small[...], -32)[0:1, 0:32]
    lane = lax.broadcasted_iota(jnp.int32, (8, 128), 1)
    for h in range(2):
        o_out[:, h * HALF : (h + 1) * HALF] = w4[h, :, GOUT0 : GOUT0 + HALF]
        for k in range(3):
            for j in range(0, 8, 2):
                c = 128 * (k // 2)
                even, odd = wq[h, j, :, c : c + 128], wq[h, j + 1, :, c : c + 128]
                sh = 64 * (k % 2)
                at = k * D + h * HALF + 64 * j
                o_qkv[:, at : at + 128] = jnp.where(lane < 64, roll(even, -sh), roll(odd, 64 - sh))
    for k in range(32):
        c = GFC0 + 128 * (k // 2)
        o_fc[:, 128 * k : 128 * k + 128] = quarters(
            [
                roll(w4[a % 2, :, c : c + 128], 32 * a - 32 * ((2 * k + a // 2) % 4))
                for a in range(4)
            ]
        )


def kernel(
    w_qkv,
    w_out,
    w_fc,
    gains,
    shifts,
    attn_biases,
    branch_biases,
    fc_bias,
    tokens,
    cot,
    wproj,
    o_block,
    o_in,
    o_w4,
    o_wq,
    o_wp,
    o_small,
    *scratch,
):
    names = list(SCRATCH)
    r = dict(zip(names, scratch[: len(names)]))
    wpack = r["pack"]
    stages = scratch[len(names) :]
    r["dkv"] = r["sbuf"].at[:, 0 : 2 * HEAD]
    r["dh1"] = r["outp"]
    r["dmid"] = r["part"]
    r["gos"] = r["wor"].at[:, :, :, :, :, 0:HALF]
    r["dqt"] = r["ot"]
    dp, sq = lax.axis_index("dp"), lax.axis_index("seq")
    core = lax.rem(sq, 2)
    me = dict(
        x=lax.div(dp, 2),
        y=lax.div(sq, 4),
        z=lax.rem(lax.div(sq, 2), 2) * 2 + lax.rem(dp, 2),
    )
    my, mz = me["y"], lax.div(me["z"], 2)
    j_me = lax.div(sq, 2)
    partner = (dp, sq + 1 - 2 * core)

    def seq_peer(t):
        jj = lax.rem(j_me + t, 8)
        return jj, (dp, jj * 2 + core)

    def dp_peer(t):
        ii = lax.rem(dp + t, 8)
        return ii, (ii, sq)

    peers = [partner, dev(shift(me, "z", 2 * lax.rem(me["z"], 2) - 1), core)]
    for t in range(1, 8):
        peers += [seq_peer(t)[1], dp_peer(t)[1]]
    bar = pltpu.get_barrier_semaphore()
    for t in peers:
        pl.semaphore_signal(bar, inc=1, device_id=t, device_id_type=MESH)
    vectors = (gains, shifts, attn_biases, branch_biases)
    pack(wpack, r["tiny"], w_qkv, w_out, w_fc, vectors, fc_bias)
    pl.semaphore_wait(bar, len(peers))

    def sems(name):
        return r[name + "_s"], r[name + "_r"]

    def pair(src, dst, i):
        return remote_copy(src, dst, sems("px"), i, partner)

    mine_rows = pl.ds(pl.multiple_of(core * 128, 128), 128)
    their_rows = pl.ds(pl.multiple_of(128 - core * 128, 128), 128)
    half0 = pl.multiple_of(core * HALF, HALF)
    half1 = pl.multiple_of(HALF - core * HALF, HALF)
    own = (me["x"], lax.rem(me["z"], 2), me["y"], mz)

    def tok(jj):
        return pl.ds(pl.multiple_of(jj * T, T), T)

    class Swap:
        def __init__(self, name, k, peer, at, send, land):
            self.name, self.k, self.peer, self.at = name, k, peer, at
            self.send, self.land = send, land

        def copy(self, t):
            pp, to = self.peer(t)
            return remote_copy(
                self.send(pp), self.land(self.at), sems(self.name), self.k * 8 + t, to
            )

        def start(self):
            for t in range(1, 8):
                self.copy(t).start()

        def wait(self):
            for t in range(1, 8):
                pp = lax.rem(self.at + 8 - t, 8)
                remote_copy(
                    self.send(pp), self.land(pp), sems(self.name), self.k * 8 + t, partner
                ).wait_recv()

        def drain(self):
            for t in range(1, 8):
                self.copy(t).wait_send()

    def seq_swap(k, send, land):
        return Swap("a2a", k, seq_peer, j_me, send, land)

    def dp_swap(k, send, land):
        return Swap("dp", k, dp_peer, dp, send, land)

    px_w = pair(wpack.at[1 - core], r["wrecv"], 0)
    px_w.start()

    lc = [
        pltpu.make_async_copy(tokens, r["x"].at[mine_rows], r["loc"].at[1]),
        pltpu.make_async_copy(cot, r["dy"].at[mine_rows], r["loc"].at[2]),
        pltpu.make_async_copy(wproj, r["wp"].at[own], r["loc"].at[3]),
    ]
    for c in lc:
        c.start()
    px_x = pair(tokens, r["x"].at[mine_rows], 1)
    px_dy = pair(cot, r["dy"].at[mine_rows], 2)

    px_w.wait_recv()
    mine, theirs = wpack[core], r["wrecv"][...]
    first = jnp.where(core == 0, mine, theirs)
    second = jnp.where(core == 0, theirs, mine)
    r["w4"][own] = jnp.concatenate([first, second], axis=0).astype(BF16)
    for c in lc:
        c.wait()

    def gathers(table, base):
        out = []
        for i, (name, c0, n, rot) in enumerate(table):
            out.append(Gather(me, core, r[name], c0, n, rot, sems("ag"), (base + i) * 12))
        return out

    ga = gathers(GATHER_A, 0)
    gb = gathers(GATHER_B, 3)
    gc = gathers(GATHER_C, 6)
    for g in ga + gb + gc:
        g.start(0)
    px_x.start()
    px_dy.start()
    for g in ga + gb + gc:
        g.forward(0)
    for g in ga:
        g.finish(0)
        g.start(1)
    for g in gb + gc:
        g.finish(0)
        g.start(1)
    for g in ga:
        g.forward(1)
    for g in ga:
        g.finish(1)
        g.start(2)
    for g in gb + gc:
        g.forward(1)
    for g in ga:
        g.forward(2)
    px_x.wait_recv()
    for g in ga:
        g.finish(2)
    for g in gb:
        g.finish(1)
        g.start(2)

    lane = lax.broadcasted_iota(jnp.int32, (8, 128), 1)
    vec_t = [jnp.zeros((8, 128), F32) for _ in range(8)]
    fcb_t = [jnp.zeros((8, 128), F32) for _ in range(16)]
    for p in range(64):
        tile = r["w4"][
            p // 16, (p // 8) % 2, (p // 2) % 4, p % 2, :, SMALL0 : SMALL0 + 128
        ].astype(F32)
        lo, hi = tile[0:8], tile[8:16]
        at = 16 * (p % 8)
        both = jnp.where(lane < 8, lo, 0.0) + pltpu.roll(jnp.where(lane < 8, hi, 0.0), 8, 1)
        vec_t[p // 8] = vec_t[p // 8] + (pltpu.roll(both, at, 1) if at else both)
        fc = jnp.where(core == 0, lo, hi)
        fc = jnp.where((lane >= 32) & (lane < 64), fc, 0.0)
        sh = (32 * (p % 4) - 32) % 128
        fcb_t[p // 4] = fcb_t[p // 4] + (pltpu.roll(fc, sh, 1) if sh else fc)
    for k in range(8):
        r["vec"][:, 128 * k : 128 * k + 128] = vec_t[k]
    for k in range(16):
        r["fcb"][:, 128 * k : 128 * k + 128] = fcb_t[k]

    def vrow(i):
        return r["vec"][i : i + 1, :]

    def ln1(rows, c):
        xhat, _ = norm_stats(r["x"][rows, :].astype(F32))
        r["h1"][rows, :] = (xhat * vrow(0) + vrow(2)).astype(BF16)
        return c

    rows_loop(T, 32, ln1)
    for k in range(3):
        w = r["w4"][:, :, :, :, :, k * HALF : (k + 1) * HALF].reshape(D, HALF)
        v = nn(r["h1"][...], w)
        if k == 0:
            v = v + r["vec"][4:5, pl.ds(half0, HALF)]
        if k == 2:
            v = v + r["vec"][5:6, pl.ds(half0, HALF)]
        r["qkvs"][k] = v.T.astype(BF16).reshape(8, HEAD, T)
    qkv_swap = seq_swap(0, lambda j: r["qkvs"].at[:, j], lambda j: r["qkvt"].at[:, :, tok(j)])
    qkv_swap.start()
    r["qkvt"][:, :, tok(j_me)] = r["qkvs"][:, j_me]
    for g in gc:
        g.finish(1)
    for g in gb:
        g.forward(2)
    for g in gc:
        g.start(2)

    def hcopy(src, dst, i, axis, d):
        return remote_copy(src, dst, sems("xg"), i, dev(shift(me, axis, d), core))

    def hrows(yy, zz, row, n):
        return r["hs"].at[yy, zz, core, pl.ds(row, n)]

    def h_from(yy, zz, row, n, i):
        ref = hrows(yy, zz, row, n)
        hcopy(ref, ref, i, "y", 1).wait_recv()

    every = slice(None)
    ym, yp, opposite = mod4(my - 1), mod4(my + 1), mod4(my + 2)
    h_z = hcopy(hrows(my, mz, 0, 128), hrows(my, mz, 0, 128), 0, "z", 2)
    h_y = [
        hcopy(hrows(my, every, 0, 128), hrows(my, every, 0, 128), 1 + way(d), "y", d)
        for d in (1, -1)
    ]
    h_f = [
        hcopy(hrows(ym, every, 0, 64), hrows(ym, every, 0, 64), 3, "y", 1),
        hcopy(hrows(yp, every, 64, 64), hrows(yp, every, 64, 64), 4, "y", -1),
    ]
    h1s = r["hs"].reshape(LEN, D)
    k_t, v_t = r["qkvt"].at[1], r["qkvt"].at[2]
    qkv_swap.wait()

    r["qz"][0:HEAD, :] = r["qkvt"][0]
    r["qz"][HEAD:, :] = jnp.zeros((HEAD, LEN), BF16)

    def to_rows(ref, parts):
        def one(i, c):
            cols = pl.ds(pl.multiple_of(i * JB, JB), JB)
            stacked = jnp.concatenate([p(cols) for p in parts], axis=0).astype(F32)
            ref[cols, :] = stacked.T.astype(BF16)
            return c

        lax.fori_loop(0, LEN // JB, one, 0)

    to_rows(r["kv"], [lambda cols: k_t[:, cols], lambda cols: v_t[:, cols]])

    row_i = lax.broadcasted_iota(jnp.int32, (JB, IB), 0)
    col_i = lax.broadcasted_iota(jnp.int32, (JB, IB), 1)

    def jcols(jb):
        return pl.ds(pl.multiple_of(jb * JB, JB), JB)

    def attend(ib, c):
        icols = pl.ds(pl.multiple_of(ib * IB, IB), IB)
        q = r["qz"][:, icols]
        nfull = lax.div(ib * IB, JB)

        def fold_max(s):
            return jnp.max(s.reshape(JB // 8, 8, IB), axis=0)

        def scores(jb, m):
            s = nn(r["kv"][jcols(jb), :], q)
            r["sbuf"][jcols(jb), :] = s
            return jnp.maximum(m, fold_max(s))

        m = lax.fori_loop(0, nfull, scores, jnp.full((8, IB), LOW, F32))
        s = nn(r["kv"][jcols(nfull), :], q)
        s = jnp.where(nfull * JB + row_i <= ib * IB + col_i, s, LOW)
        r["sbuf"][jcols(nfull), :] = s
        m = jnp.max(jnp.maximum(m, fold_max(s)), axis=0, keepdims=True) * SCALE2

        def weigh(jb, state):
            l, o = state
            p = jnp.exp2(r["sbuf"][jcols(jb), :] * SCALE2 - m)
            l = l + fold8(p)
            return l, o + nn(v_t[:, jcols(jb)], p.astype(BF16))

        l, o = lax.fori_loop(
            0, nfull + 1, weigh, (jnp.zeros((8, IB), F32), jnp.zeros((HEAD, IB), F32))
        )
        l = jnp.sum(l, axis=0, keepdims=True)
        o = o / l
        r["ot"][:, icols] = o
        r["ots"][:, icols] = o.astype(BF16)
        r["lse"][:, icols] = jnp.broadcast_to(m + jnp.log2(l), (8, IB))

        @pl.when(ib == 5)
        def _():
            for g in gc:
                g.forward(2)

        return c

    lax.fori_loop(0, LEN // IB, attend, 0)
    att_swap = seq_swap(1, lambda j: r["ots"].at[:, tok(j)], lambda j: r["attt"].at[j])
    att_swap.start()
    r["attt"][j_me] = r["ots"][:, tok(j_me)]
    for g in gb:
        g.finish(2)
    keep = r["w4"].at[pl.ds(2 * core, 2), :, :, :, :, pl.ds(OUT0, HALF)]
    give = r["w4"].at[pl.ds(2 - 2 * core, 2), :, :, :, :, pl.ds(OUT0, HALF)]
    wor_mine = r["wor"].at[:, :, :, :, :, pl.ds(half0, HALF)]
    px_wo = pair(give, wor_mine, 3)
    px_wo.start()
    lc_wo = pltpu.make_async_copy(keep, wor_mine, r["loc"].at[4])
    lc_wo.start()
    lc_h = pltpu.make_async_copy(r["h1"].at[mine_rows], r["hs"].at[my, mz, core], r["loc"].at[5])
    lc_h.start()
    lc_h.wait()
    h_z.start()
    att_swap.wait()
    lc_wo.wait()
    px_wo.wait_recv()

    att = r["attt"][...].reshape(8 * HEAD, T).astype(F32).T.astype(BF16)
    r["part"][...] = nn(att, r["wor"][...].reshape(HALF, D))
    px_p = pair(r["part"], r["partr"], 4)
    px_p.start()
    px_p.wait()

    def ln2(rows, c):
        mid = r["x"][rows, :].astype(F32) + (r["part"][rows, :] + r["partr"][rows, :] + vrow(6))
        r["middle"][rows, :] = mid
        xhat, _ = norm_stats(mid)
        r["h2"][rows, :] = (xhat * vrow(1) + vrow(3)).astype(BF16)
        return c

    rows_loop(T, 32, ln2)
    r["h2t"][...] = r["h2"][...].astype(F32).T.astype(BF16)
    px_dy.wait_recv()
    h_from(my, 1 - mz, 0, 128, 0)
    for c in h_y:
        c.start()
    for g in gc:
        g.finish(2)

    def ffn(t, c):
        hi, lo = lax.div(t, 2), lax.rem(t, 2)
        cols = pl.ds(pl.multiple_of(t * 256, 256), 256)
        wf = r["w4"][:, :, :, :, :, pl.ds(pl.multiple_of(FC0 + t * 256, 128), 256)].reshape(D, 256)
        wp = r["wp"][hi, lo].reshape(256, D)
        pre = nn(r["h2"][...], wf) + r["fcb"][0:1, cols]
        d_act = nt(r["dy"][...], wp)
        sq_ = pre * pre
        th = jnp.tanh(0.7978845608028654 * (pre + 0.044715 * sq_ * pre))
        act = 0.5 * pre * (1.0 + th)
        slope = 0.5 * (1.0 + th) + 0.5 * pre * (1.0 - th * th) * (
            0.7978845608028654 * (1.0 + 3.0 * 0.044715 * sq_)
        )
        d_pre = (slope * d_act).astype(BF16)
        r["act"][:, cols] = act.astype(BF16)
        r["dpre"][:, cols] = d_pre
        r["sfc"][:, cols] = jnp.broadcast_to(
            jnp.sum(d_pre.astype(F32), axis=0, keepdims=True), (8, 256)
        )

        return c

    lax.fori_loop(0, 8, ffn, 0)

    def ffn_dh(n, c):
        cols = pl.ds(pl.multiple_of(n * 256, 256), 256)
        r["dh"][:, cols] = nt(r["dpre"][...], r["w4"][n, :, :, :, :, FC0:].reshape(256, FFH))
        return c

    lax.fori_loop(0, 4, ffn_dh, 0)
    px_dh = pair(r["dh"], r["dhr"], 5)
    px_dh.start()

    def reduces(table, base, stage_at):
        out = []
        for i, (name, c0, n, rot) in enumerate(table):
            piece = Reduce(me, core, r[name], c0, n, rot, sems("rs"), (base + i) * 12)
            k = (stage_at + i) * 9
            out.append(piece.attach(stages[k : k + 9]))
        return out

    rp = reduces(REDUCE_P, 0, 0)
    rf = reduces(REDUCE_F, 2, 2)
    ro = reduces(REDUCE_O, 6, 6)

    def grad_proj(t, c):
        hi, lo = lax.div(t, 2), lax.rem(t, 2)
        cols = pl.ds(pl.multiple_of(t * 256, 256), 256)
        act_t = r["act"][:, cols].astype(F32).T.astype(BF16)
        r["gp"][hi, lo] = nn(act_t, r["dy"][...]).astype(BF16).reshape(4, 2, 32, D)
        return c

    lax.fori_loop(0, 8, grad_proj, 0)
    for g in rp:
        g.start(0)

    r["sv"][...] = jnp.zeros((8, D), F32)
    px_dh.wait_recv()

    def ln2_back(rows, c):
        dh = r["dh"][rows, :] + r["dhr"][rows, :]
        r["dhr"][rows, :] = dh
        xhat, inv = norm_stats(r["middle"][rows, :])
        d_mid = r["dy"][rows, :].astype(F32) + norm_back(xhat, inv, dh, vrow(1))
        r["dmid"][rows, :] = d_mid
        r["dbr"][rows, :] = d_mid.astype(BF16)
        return c

    rows_loop(T, 32, ln2_back)

    wor = r["wor"][...].reshape(HALF, D)
    r["datt"][...] = nt(wor, r["dbr"][...]).astype(BF16).reshape(8, HEAD, T)

    datt_swap = seq_swap(
        2, lambda j: r["datt"].at[j], lambda j: r["dz"].at[pl.ds(HEAD, HEAD), tok(j)]
    )
    datt_swap.start()
    r["dz"][HEAD:, tok(j_me)] = r["datt"][j_me]
    r["dz"][0:HEAD, :] = jnp.zeros((HEAD, LEN), BF16)

    def grad_fc(t, c):
        cols = pl.ds(pl.multiple_of(GFC0 + t * 256, 256), 256)
        r["g4"][:, :, :, :, :, cols] = (
            nn(r["h2t"][...], r["dpre"][:, pl.ds(pl.multiple_of(t * 256, 256), 256)])
            .astype(BF16)
            .reshape(4, 2, 4, 2, 16, 256)
        )
        return c

    lax.fori_loop(0, 8, grad_fc, 0)
    for g in rf:
        g.start(0)

    def ffn_out(n, c):
        cols = pl.ds(pl.multiple_of(n * 256, 256), 256)
        r["outp"][:, cols] = nn(r["act"][...], r["wp"][:, :, :, :, :, cols].reshape(FFH, 256))
        return c

    lax.fori_loop(0, 4, ffn_out, 0)
    px_out = pair(r["outp"].at[their_rows], r["outr"], 6)
    px_out.start()

    gout = nn(r["attt"][...].reshape(HALF, T), r["dbr"][...]).astype(BF16)
    left = gout[:, :HALF].reshape(2, 2, 4, 2, 16, HALF)
    right = gout[:, HALF:].reshape(2, 2, 4, 2, 16, HALF)
    go_at = r["g4"].at[pl.ds(2 * core, 2), :, :, :, :, pl.ds(GOUT0, HALF)]
    go_at[...] = jnp.where(core == 0, left, right)
    r["gos"][...] = jnp.where(core == 0, right, left)
    px_go = pair(r["gos"], go_at, 7)
    px_go.start()

    def small2(i, c):
        s1, s2, s3, s4 = c
        rows = pl.ds(pl.multiple_of(core * 128 + i * 32, 32), 32)
        dh = r["dhr"][rows, :]
        xhat, _ = norm_stats(r["middle"][rows, :])
        return (
            s1 + fold8(dh * xhat),
            s2 + fold8(dh),
            s3 + fold8(r["dbr"][rows, :].astype(F32)),
            s4 + fold8(r["dy"][rows, :].astype(F32)),
        )

    zero = jnp.zeros((8, D), F32)
    sums = lax.fori_loop(0, 4, small2, (zero, zero, zero, zero))
    for row, s in zip((1, 3, 6, 7), sums):
        r["sv"][row : row + 1, :] = jnp.sum(s, axis=0, keepdims=True)

    px_out.wait_recv()

    def block_out(i, c):
        rows = pl.ds(pl.multiple_of(core * 128 + i * 32, 32), 32)
        here = pl.ds(pl.multiple_of(i * 32, 32), 32)
        o_block[here, :] = (
            r["middle"][rows, :] + (r["outp"][rows, :] + r["outr"][here, :]) + vrow(7)
        ).astype(BF16)
        return c

    lax.fori_loop(0, 4, block_out, 0)
    px_out.wait_send()

    h_from(ym, every, 0, 128, 1)
    h_f[0].start()
    h_from(yp, every, 0, 128, 2)
    h_f[1].start()
    px_go.wait_recv()
    for g in ro:
        g.start(0)
    for g in rp:
        g.forward(0)
    datt_swap.wait()

    to_rows(r["qd"], [lambda cols: r["qz"][0:HEAD, cols], lambda cols: r["dz"][HEAD:, cols]])
    r["rowdot"][...] = jnp.broadcast_to(
        jnp.sum(r["dz"][HEAD:, :].astype(F32) * r["ot"][...], axis=0, keepdims=True), (8, LEN)
    )
    r["dkv"][...] = jnp.zeros((LEN, 2 * HEAD), F32)
    lane_kv = lax.broadcasted_iota(jnp.int32, (JB, 2 * HEAD), 1)

    px_h = pair(r["hs"].at[:, :, core], r["hs"].at[:, :, core], 12)

    def attend_back(ib, c):
        icols = pl.ds(pl.multiple_of(ib * IB, IB), IB)
        q, do = r["qz"][:, icols], r["dz"][:, icols]
        qd = r["qd"][icols, :]
        lse, dot = r["lse"][0:1, icols], r["rowdot"][0:1, icols]
        nfull = lax.div(ib * IB, JB)

        def step(jb, dq, masked):
            kv = r["kv"][jcols(jb), :]
            p = jnp.exp2(nn(kv, q) * SCALE2 - lse)
            if masked:
                p = jnp.where(jb * JB + row_i <= ib * IB + col_i, p, 0.0)
            ds = (p * (nn(kv, do) - dot)).astype(BF16)
            r["dkv"][jcols(jb), :] += jnp.where(
                lane_kv < HEAD, nn(ds, qd), nn(p.astype(BF16), qd)
            )
            return dq + nn(k_t[:, jcols(jb)], ds)

        dq = lax.fori_loop(
            0, nfull, lambda jb, a: step(jb, a, False), jnp.zeros((HEAD, IB), F32)
        )
        r["dqt"][:, icols] = step(nfull, dq, True)

        @pl.when(ib == 2)
        def _():
            rf[0].forward(0)

        @pl.when(ib == 6)
        def _():
            h_from(opposite, every, 0, 64, 3)
            h_from(opposite, every, 64, 64, 4)
            px_h.start()

        @pl.when(ib == 5)
        def _():
            for g in rf[1:] + ro:
                g.forward(0)

        return c

    lax.fori_loop(0, LEN // IB, attend_back, 0)

    r["dqkvt"][0] = (r["dqt"][...] * 0.125).astype(BF16)

    def kv_back(jb, c):
        both = r["dkv"][jcols(jb), :].T
        r["dqkvt"][1, :, jcols(jb)] = (both[:HEAD] * 0.125).astype(BF16)
        r["dqkvt"][2, :, jcols(jb)] = both[HEAD:].astype(BF16)
        return c

    lax.fori_loop(0, LEN // JB, kv_back, 0)

    dqkv_swap = seq_swap(3, lambda j: r["dqkvt"].at[:, :, tok(j)], lambda j: r["dqs"].at[:, j])
    dqkv_swap.start()
    r["dqs"][:, j_me] = r["dqkvt"][:, :, tok(j_me)]

    px_h.wait_recv()
    d192 = r["dqkvt"][...].reshape(3 * HEAD, LEN)
    for k in range(4):
        g = nn(d192, h1s[:, 256 * k : 256 * k + 256]).astype(BF16)
        r["gqs"][2 * k] = g[:, :128]
        r["gqs"][2 * k + 1] = g[:, 128:]
    gq_swap = dp_swap(1, lambda i: r["gqs"].at[i], lambda i: r["gqr"].at[i])
    gq_swap.start()
    r["gqr"][dp] = r["gqs"][dp]
    for g in rp:
        g.finish(0)
        g.start(1)
    for g in rf[:1]:
        g.finish(0)
        g.start(1)
    for g in rp:
        g.forward(1)
    dqkv_swap.wait()

    for k in range(3):
        d = r["dqs"][k].reshape(HALF, T).astype(F32).T
        if k != 1:
            row = 4 if k == 0 else 5
            r["sv"][row : row + 1, pl.ds(half0, HALF)] = jnp.sum(d, axis=0, keepdims=True)
        w = r["w4"][:, :, :, :, :, k * HALF : (k + 1) * HALF].reshape(D, HALF)
        v = nt(d.astype(BF16), w)
        r["dh1"][...] = v if k == 0 else r["dh1"][...] + v
    px_d1 = pair(r["dh1"].at[their_rows], r["dh1r"], 8)
    px_d1.start()
    for g in rf[:1]:
        g.forward(1)
    for g in rf[1:] + ro:
        g.finish(0)
        g.start(1)
    for g in rp:
        g.finish(1)
        g.start(2)
    gq_swap.wait()
    total = r["gqr"][0].astype(F32)
    for i in range(1, 8):
        total = total + r["gqr"][i].astype(F32)
    total = jnp.concatenate([total, jnp.zeros((HEAD, 128), F32)], axis=0)
    r["gqt"][...] = total.T.reshape(8, 16, 256)
    gqt_swap = seq_swap(4, lambda j: r["gqt"].at[j], lambda j: r["finq"].at[j])
    gqt_swap.start()
    r["finq"][j_me] = r["gqt"][j_me]
    for g in rf[:1]:
        g.finish(1)
        g.start(2)
    for g in rf[1:] + ro:
        g.forward(1)
    for g in rp:
        g.forward(2)
    px_d1.wait_recv()

    def ln1_back(i, c):
        s1, s2 = c
        rows = pl.ds(pl.multiple_of(core * 128 + i * 32, 32), 32)
        here = pl.ds(pl.multiple_of(i * 32, 32), 32)
        dh = r["dh1"][rows, :] + r["dh1r"][here, :]
        xhat, inv = norm_stats(r["x"][rows, :].astype(F32))
        d_in = r["dmid"][rows, :] + norm_back(xhat, inv, dh, vrow(0))
        o_in[here, :] = d_in.astype(BF16)
        return s1 + fold8(dh * xhat), s2 + fold8(dh)

    sums = lax.fori_loop(0, 4, ln1_back, (zero, zero))
    for row, s in zip((0, 2), sums):
        r["sv"][row : row + 1, :] = jnp.sum(s, axis=0, keepdims=True)

    for i in range(8):
        r["ss"][i, 0:8] = r["sv"][:, 128 * i : 128 * i + 128]
        r["ss"][i, 8:9] = r["sfc"][0:1, 256 * i : 256 * i + 128]
        r["ss"][i, 9:10] = r["sfc"][0:1, 256 * i + 128 : 256 * i + 256]
        r["ss"][i, 10:16] = jnp.zeros((6, 128), F32)
    ss_swap = dp_swap(2, lambda i: r["ss"].at[i], lambda i: r["ssr"].at[i])
    ss_swap.start()
    r["ssr"][dp] = r["ss"][dp]
    for g in rf[1:] + ro:
        g.finish(1)
        g.start(2)
    for g in rf[:1]:
        g.forward(2)
    ss_swap.wait()
    r["st"][...] = jnp.sum(r["ssr"][...], axis=0)
    st_swap = seq_swap(5, lambda j: r["st"], lambda j: r["str"].at[j])
    st_swap.start()
    r["str"][j_me] = r["st"][...]

    mine8 = pl.ds(pl.multiple_of(core * 8, 8), 8)
    their8 = pl.ds(pl.multiple_of(8 - core * 8, 8), 8)
    for g in rf[1:] + ro:
        g.forward(2)
    gqt_swap.wait()
    px_q = pair(r["finq"].at[:, their8], o_wq.at[core], 11)
    px_q.start()
    o_wq[core] = r["finq"][:, mine8, :]
    for g in rp + rf + ro:
        tall = g.ref is r["gp"]
        g.finish(2, (o_wp if tall else r["fin"]).at[:, pl.ds(g.c0, g.n)])
    px_f = pair(r["fin"].at[their8], o_w4.at[core], 9)
    px_f.start()
    o_w4[core] = r["fin"][mine8, :]
    st_swap.wait()
    r["fins"][...] = jnp.sum(r["str"][...], axis=0)
    px_s = pair(r["fins"], r["finr"], 10)
    px_s.start()
    px_s.wait_recv()
    total = r["fins"][0:8, :] + r["finr"][0:8, :]
    total = pltpu.roll(total, lax.rem(128 - (16 * j_me + 8 * core), 128), 1)
    fc = jnp.where(lax.div(j_me, 4) == 0, r["fins"][8:9, :], r["fins"][9:10, :])
    fc = pltpu.roll(jnp.broadcast_to(fc, (8, 128)), lax.rem(160 - 32 * lax.rem(j_me, 4), 128), 1)
    o_small[...] = jnp.where(lane < 8, total, fc)
    px_q.wait_recv()
    px_f.wait_recv()

    for g in ga + gb + gc + rp + rf + ro:
        g.drain()
    for g in (qkv_swap, att_swap, datt_swap, dqkv_swap, gq_swap, gqt_swap, ss_swap, st_swap):
        g.drain()
    for c in (px_w, px_x, px_dy, px_wo, px_dh, px_go, px_d1, px_q, px_f, px_s, px_h, h_z, *h_y, *h_f):
        c.wait_send()


def stage_list():
    out = []
    for name, _, n, rot in REDUCE_P + REDUCE_F + REDUCE_O:
        out += Reduce.stage_shapes(ROWS[name], n, rot, BF16)
    return out


def block(*args):
    vm = pl.BlockSpec(memory_space=pltpu.VMEM)
    return pl.pallas_call(
        kernel,
        out_shape=(
            jax.ShapeDtypeStruct((128, D), BF16),
            jax.ShapeDtypeStruct((128, D), BF16),
            jax.ShapeDtypeStruct((2, 8, G4), F32),
            jax.ShapeDtypeStruct((2, 8, 8, 256), F32),
            jax.ShapeDtypeStruct((32, D), F32),
            jax.ShapeDtypeStruct((8, 128), F32),
        ),
        in_specs=[vm] * len(args),
        out_specs=(vm,) * 6,
        scratch_shapes=list(SCRATCH.values()) + stage_list(),
        compiler_params=pltpu.CompilerParams(
            collective_id=0, has_side_effects=True, vmem_limit_bytes=63 * 2**20
        ),
    )(*args)


def outputs(*results):
    vm = pl.BlockSpec(memory_space=pltpu.VMEM)
    vector = jax.ShapeDtypeStruct((2, 8), F32)
    return pl.pallas_call(
        unpack,
        out_shape=(
            jax.ShapeDtypeStruct((128, D), BF16),
            jax.ShapeDtypeStruct((128, D), BF16),
            vector,
            vector,
            jax.ShapeDtypeStruct((8, 3 * D), F32),
            vector,
            jax.ShapeDtypeStruct((8, D), F32),
            vector,
            jax.ShapeDtypeStruct((8, FF), F32),
            jax.ShapeDtypeStruct((1, 32), F32),
            jax.ShapeDtypeStruct((32, D), F32),
        ),
        in_specs=[vm] * len(results),
        out_specs=(vm,) * 11,
    )(*results)


def on_device(
    tokens,
    norm_gains,
    norm_biases,
    w_qkv,
    attn_biases,
    w_out,
    branch_biases,
    w_fc,
    fc_bias,
    w_proj,
    cotangent,
):
    results = block(
        w_qkv,
        w_out,
        w_fc,
        norm_gains,
        norm_biases,
        attn_biases,
        branch_biases,
        fc_bias[None],
        tokens[0],
        cotangent[0],
        w_proj,
    )
    block_out, input_grad, gains, shifts, qkv, attn, out, branch, fc, fcb, proj = outputs(*results)
    return (
        block_out[None],
        input_grad[None],
        gains,
        shifts,
        qkv,
        attn,
        out,
        branch,
        fc,
        fcb[0],
        proj,
    )


def solution(mesh):
    in_specs = (
        P("dp", "seq", None),
        P(None, ("dp", "seq")),
        P(None, ("dp", "seq")),
        P(("dp", "seq"), None),
        P(None, ("dp", "seq")),
        P(("dp", "seq"), None),
        P(None, ("dp", "seq")),
        P(("dp", "seq"), None),
        P(("dp", "seq")),
        P(("dp", "seq"), None),
        P("dp", "seq", None),
    )
    out_specs = (
        P("dp", "seq", None),
        P("dp", "seq", None),
        P(None, ("dp", "seq")),
        P(None, ("dp", "seq")),
        P(("dp", "seq"), None),
        P(None, ("dp", "seq")),
        P(("dp", "seq"), None),
        P(None, ("dp", "seq")),
        P(("dp", "seq"), None),
        P(("dp", "seq")),
        P(("dp", "seq"), None),
    )
    return jax.shard_map(
        on_device, mesh=mesh, in_specs=in_specs, out_specs=out_specs, check_vma=False
    )
```

```python
import functools
import math

import jax
import jax.numpy as jnp
from jax import lax
from jax.experimental import pallas as pl
from jax.experimental.pallas import tpu as pltpu
from jax.sharding import PartitionSpec as P

MESH = pl.DeviceIdType.MESH
BF16 = jnp.bfloat16
F32 = jnp.float32

H = 16
HEAD = 64
D = 1024
FF = 4096
T = 256
LEN = 2048
HALF = D // 2
FFH = FF // 2
EPS = 1e-05
LOW = -1e30
SCALE2 = math.log2(math.e) / math.sqrt(HEAD)

SMALL0 = 3 * HALF
OUT0 = SMALL0 + 128
FC0 = OUT0 + HALF
W4 = FC0 + FFH
GOUT0 = 0
GFC0 = HALF
G4 = GFC0 + FFH

JB = 512
IB = 256

ORDERS = (("x", "y", "z"), ("y", "z", "x"), ("z", "x", "y"))
SIZES = {"x": 4, "y": 4, "z": 4}


def nt(a, b):
    return lax.dot_general(a, b, (((1,), (1,)), ((), ())), preferred_element_type=F32)


def nn(a, b):
    return jnp.dot(a, b, preferred_element_type=F32)


def mod4(v):
    return lax.rem(v + 4, 4)


def dev(co, core):
    x, y, z = co["x"], co["y"], co["z"]
    return (x * 2 + lax.rem(z, 2), y * 4 + lax.div(z, 2) * 2 + core)


def shift(co, axis, d):
    out = dict(co)
    out[axis] = mod4(co[axis] + d)
    return out


def blocks(ref, sel, c0, n):
    s = slice(None)
    x, y, z = sel["x"], sel["y"], sel["z"]
    return ref.at[
        s if x is None else x,
        s if z is None else lax.rem(z, 2),
        s if y is None else y,
        s if z is None else lax.div(z, 2),
        :,
        pl.ds(c0, n),
    ]


def lead_dims(fixed):
    out = []
    if "x" not in fixed:
        out.append(4)
    if "z" not in fixed:
        out.append(2)
    if "y" not in fixed:
        out.append(4)
    if "z" not in fixed:
        out.append(2)
    return tuple(out)


def half_split(n):
    first = ((n // 128) + 1) // 2 * 128
    return ((0, first), (first, n - first))


def way(d):
    return 0 if d > 0 else 1


def remote_copy(src, dst, sems, i, to):
    return pltpu.make_async_remote_copy(
        src_ref=src,
        dst_ref=dst,
        send_sem=sems[0].at[i],
        recv_sem=sems[1].at[i],
        device_id=to,
        device_id_type=MESH,
    )


ring_copy = remote_copy


class Piece:
    def __init__(self, me, core, ref, c0, n, rot, sems, base):
        self.me, self.core, self.ref, self.c0, self.n = me, core, ref, c0, n
        self.order = ORDERS[rot]
        self.sems, self.base = sems, base

    def cols(self, h):
        if h is None:
            return self.c0, self.n
        off, n = half_split(self.n)[h]
        return self.c0 + off, n

    def remote(self, src, dst, ph, st, d):
        to = dev(shift(self.me, self.order[ph], d), self.core)
        return ring_copy(src, dst, self.sems, self.base + ph * 4 + st * 2 + way(d), to)


class Gather(Piece):
    def region(self, ph, off, h):
        sel = {}
        for k, a in enumerate(self.order):
            sel[a] = None if k < ph else (mod4(self.me[a] + off) if k == ph else self.me[a])
        return blocks(self.ref, sel, *self.cols(h))

    direct = (0,)

    def ways1(self):
        return (1, -1) if self.n > 128 else (1,)

    def copy(self, ph, st, d):
        r = self.region(ph, 0, None) if st == 0 else self.region(ph, -d, way(d))
        return self.remote(r, r, ph, st, d)

    def across(self, ph, off):
        r = self.region(ph, off, None)
        return self.remote(r, r, ph, 1, 2)

    def start(self, ph):
        for d in (1, -1):
            self.copy(ph, 0, d).start()
        if ph in self.direct:
            self.across(ph, 0).start()

    def forward(self, ph):
        if ph in self.direct:
            return
        for d in (1, -1):
            r = self.region(ph, -d, None)
            self.remote(r, r, ph, 0, d).wait_recv()
            if d in self.ways1():
                self.copy(ph, 1, d).start()

    def finish(self, ph):
        if ph in self.direct:
            for d in (1, -1):
                r = self.region(ph, -d, None)
                self.remote(r, r, ph, 0, d).wait_recv()
            self.across(ph, 2).wait_recv()
            return
        for d in self.ways1():
            r = self.region(ph, -2 * d, way(d))
            self.remote(r, r, ph, 1, d).wait_recv()

    def drain(self):
        for ph in range(3):
            for d in (1, -1):
                self.copy(ph, 0, d).wait_send()
            if ph in self.direct:
                self.across(ph, 0).wait_send()
            else:
                for d in self.ways1():
                    self.copy(ph, 1, d).wait_send()


class Reduce(Piece):
    def attach(self, stage):
        self.stage = stage
        return self

    @staticmethod
    def stage_shapes(rows, n, rot, dtype):
        (_, n0), (_, n1) = half_split(n)
        lead = [lead_dims(ORDERS[rot][: ph + 1]) for ph in range(3)]
        return [
            pltpu.VMEM(lead[0] + (rows, n0), dtype),
            pltpu.VMEM(lead[0] + (rows, n1), dtype),
            pltpu.VMEM((2,) + lead[0] + (rows, n), dtype),
            pltpu.VMEM((3,) + lead[1] + (rows, n), dtype),
            pltpu.VMEM((3,) + lead[2] + (rows, n), dtype),
        ]

    def region(self, ph, off, h):
        sel = {}
        for k, a in enumerate(self.order):
            sel[a] = self.me[a] if k < ph else (mod4(self.me[a] + off) if k == ph else None)
        return blocks(self.ref, sel, *self.cols(h))

    def copy(self, ph, st, d):
        if st == 0:
            return self.remote(self.region(ph, 2, way(d)), self.stage[way(d)], ph, 0, d)
        return self.remote(self.region(ph, d, None), self.stage[2].at[way(d)], ph, 1, d)

    def straight(self, ph, k):
        d = (1, -1, 2)[k]
        st = 1 if k == 2 else 0
        return self.remote(self.region(ph, d, None), self.stage[2 + ph].at[k], ph, st, d)

    def start(self, ph):
        if ph:
            for k in range(3):
                self.straight(ph, k).start()
        else:
            for d in (1, -1):
                self.copy(0, 0, d).start()

    def add(self, target, sources, lead, wide=False):
        def one(idx):
            total = target[idx].astype(F32) if wide else target[idx]
            for s in sources:
                total = total + s[idx].astype(total.dtype)
            target[idx] = total.astype(target.dtype)

        if not lead:
            one(Ellipsis)
        else:
            lax.fori_loop(0, lead[0], lambda i, c: (one(i), c)[1], 0)

    def forward(self, ph):
        if ph:
            return
        lead = lead_dims(self.order[:1])
        for d in (1, -1):
            self.copy(0, 0, d).wait_recv()
            self.add(self.region(0, d, way(d)), [self.stage[way(d)]], lead)
            self.copy(0, 1, d).start()

    def finish(self, ph, out=None):
        lead = lead_dims(self.order[: ph + 1])
        s = self.stage[2 + ph]
        if ph:
            for k in range(3):
                self.straight(ph, k).wait_recv()
        else:
            for d in (1, -1):
                self.copy(0, 1, d).wait_recv()
        mine = self.region(ph, 0, None)
        arrived = [s.at[k] for k in range(3 if ph else 2)]
        if out is None:
            self.add(mine, arrived, lead, wide=ph > 0)
        else:
            total = mine[...].astype(F32)
            for a in arrived:
                total = total + a[...].astype(F32)
            out[...] = total

    def drain(self):
        for d in (1, -1):
            self.copy(0, 0, d).wait_send()
            self.copy(0, 1, d).wait_send()
        for ph in (1, 2):
            for k in range(3):
                self.straight(ph, k).wait_send()


GATHER_B = (
    ("w4", OUT0, HALF + 256, 0),
    ("w4", FC0 + 256, 768, 1),
    ("w4", FC0 + 1024, 768, 2),
)
GATHER_C = (
    ("w4", FC0 + 1792, 256, 0),
    ("wp", 0, 256, 0),
    ("wp", 256, 384, 1),
    ("wp", 640, 384, 2),
)
GATHER_A = (("w4", 0, HALF, 0), ("w4", HALF, HALF, 1), ("w4", 2 * HALF, HALF + 128, 2))
REDUCE_P = (("gp", 0, HALF, 1), ("gp", HALF, HALF, 2))
REDUCE_F = (
    ("g4", GFC0, 640, 0),
    ("g4", GFC0 + 640, 640, 0),
    ("g4", GFC0 + 1280, 256, 1),
    ("g4", GFC0 + 1536, HALF, 2),
)
REDUCE_O = (("g4", GOUT0, HALF, 0),)
ROWS = {"g4": 16, "gp": 32}


def rows_loop(total, step, body, init=0):
    def one(i, c):
        return body(pl.ds(pl.multiple_of(i * step, step), step), c)

    return lax.fori_loop(0, total // step, one, init)


def fold8(v):
    return jnp.sum(v.reshape(v.shape[0] // 8, 8, v.shape[1]), axis=0)


def norm_stats(v):
    average = jnp.mean(v, axis=-1, keepdims=True)
    centred = v - average
    variance = jnp.mean(centred * centred, axis=-1, keepdims=True)
    inv = lax.rsqrt(variance + EPS)
    return centred * inv, inv


def norm_back(xhat, inv, dh, gain):
    a = dh * gain
    return inv * (
        a - jnp.mean(a, axis=-1, keepdims=True) - xhat * jnp.mean(a * xhat, axis=-1, keepdims=True)
    )


SCRATCH = dict(
    w4=pltpu.VMEM((4, 2, 4, 2, 16, W4), BF16),
    wp=pltpu.VMEM((4, 2, 4, 2, 32, D), BF16),
    g4=pltpu.VMEM((4, 2, 4, 2, 16, G4), BF16),
    gp=pltpu.VMEM((4, 2, 4, 2, 32, D), BF16),
    pack=pltpu.VMEM((2, 8, W4), F32),
    tiny=pltpu.VMEM((2, 8, 128), F32),
    wrecv=pltpu.VMEM((8, W4), F32),
    wor=pltpu.VMEM((2, 2, 4, 2, 16, D), BF16),
    hs=pltpu.VMEM((4, 2, 2, 128, D), BF16),
    h1=pltpu.VMEM((T, D), BF16),
    qkvs=pltpu.VMEM((3, 8, HEAD, T), BF16),
    qkvt=pltpu.VMEM((3, HEAD, LEN), BF16),
    x=pltpu.VMEM((T, D), BF16),
    dy=pltpu.VMEM((T, D), BF16),
    h2=pltpu.VMEM((T, D), BF16),
    h2t=pltpu.VMEM((D, T), BF16),
    vec=pltpu.VMEM((8, D), F32),
    fcb=pltpu.VMEM((8, FFH), F32),
    qz=pltpu.VMEM((2 * HEAD, LEN), BF16),
    dz=pltpu.VMEM((2 * HEAD, LEN), BF16),
    kv=pltpu.VMEM((LEN, 2 * HEAD), BF16),
    qd=pltpu.VMEM((LEN, 2 * HEAD), BF16),
    sbuf=pltpu.VMEM((LEN, IB), F32),
    ot=pltpu.VMEM((HEAD, LEN), F32),
    ots=pltpu.VMEM((HEAD, LEN), BF16),
    lse=pltpu.VMEM((8, LEN), F32),
    rowdot=pltpu.VMEM((8, LEN), F32),
    attt=pltpu.VMEM((8, HEAD, T), BF16),
    act=pltpu.VMEM((T, FFH), BF16),
    dpre=pltpu.VMEM((T, FFH), BF16),
    part=pltpu.VMEM((T, D), F32),
    partr=pltpu.VMEM((T, D), F32),
    middle=pltpu.VMEM((T, D), F32),
    outp=pltpu.VMEM((T, D), F32),
    outr=pltpu.VMEM((T // 2, D), F32),
    dh=pltpu.VMEM((T, D), F32),
    dhr=pltpu.VMEM((T, D), F32),
    dbr=pltpu.VMEM((T, D), BF16),
    datt=pltpu.VMEM((8, HEAD, T), BF16),
    dqkvt=pltpu.VMEM((3, HEAD, LEN), BF16),
    dqs=pltpu.VMEM((3, 8, HEAD, T), BF16),
    dh1r=pltpu.VMEM((T // 2, D), F32),
    gqs=pltpu.VMEM((8, 3 * HEAD, 128), BF16),
    gqr=pltpu.VMEM((8, 3 * HEAD, 128), BF16),
    gqt=pltpu.VMEM((8, 16, 256), F32),
    finq=pltpu.VMEM((8, 16, 256), F32),
    sv=pltpu.VMEM((8, D), F32),
    sfc=pltpu.VMEM((8, FFH), F32),
    ss=pltpu.VMEM((8, 16, 128), F32),
    ssr=pltpu.VMEM((8, 16, 128), F32),
    st=pltpu.VMEM((16, 128), F32),
    str=pltpu.VMEM((8, 16, 128), F32),
    fin=pltpu.VMEM((16, G4), F32),
    fins=pltpu.VMEM((16, 128), F32),
    finr=pltpu.VMEM((16, 128), F32),
    ag_s=pltpu.SemaphoreType.DMA((12 * 10,)),
    ag_r=pltpu.SemaphoreType.DMA((12 * 10,)),
    rs_s=pltpu.SemaphoreType.DMA((12 * 7,)),
    rs_r=pltpu.SemaphoreType.DMA((12 * 7,)),
    xg_s=pltpu.SemaphoreType.DMA((6,)),
    xg_r=pltpu.SemaphoreType.DMA((6,)),
    a2a_s=pltpu.SemaphoreType.DMA((48,)),
    a2a_r=pltpu.SemaphoreType.DMA((48,)),
    dp_s=pltpu.SemaphoreType.DMA((24,)),
    dp_r=pltpu.SemaphoreType.DMA((24,)),
    px_s=pltpu.SemaphoreType.DMA((16,)),
    px_r=pltpu.SemaphoreType.DMA((16,)),
    loc=pltpu.SemaphoreType.DMA((8,)),
)


def roll(v, shift):
    shift %= 128
    return pltpu.roll(v, shift, 1) if shift else v


def quarters(pieces):
    lane = lax.broadcasted_iota(jnp.int32, (8, 128), 1)
    low = jnp.where(lane < 32, pieces[0], pieces[1])
    high = jnp.where(lane < 96, pieces[2], pieces[3])
    return jnp.where(lane < 64, low, high)


def pack(pack_ref, tiny, w_qkv, w_out, w_fc, vectors, fc_bias):
    q, o, f = w_qkv[...].astype(F32), w_out[...].astype(F32), w_fc[...].astype(F32)
    lane = lax.broadcasted_iota(jnp.int32, (8, 128), 1)
    tiny[...] = jnp.zeros((2, 8, 128), F32)
    for i, v in enumerate(vectors):
        tiny[0, 2 * i : 2 * i + 2, 0:8] = v[...].astype(F32)
    tiny[1, 0:1, 0:32] = fc_bias[...].astype(F32)
    small = jnp.where(lane < 8, tiny[0], roll(tiny[1], 32))
    for h in range(2):
        for k in range(3):
            c = k * D + h * HALF
            pack_ref[h, :, k * HALF : (k + 1) * HALF] = q[:, c : c + HALF]
        pack_ref[h, :, SMALL0 : SMALL0 + 128] = small
        pack_ref[h, :, OUT0 : OUT0 + HALF] = o[:, h * HALF : (h + 1) * HALF]
        for m in range(16):
            first = f[:, 256 * m : 256 * m + 128]
            second = f[:, 256 * m + 128 : 256 * m + 256]
            pack_ref[h, :, FC0 + 128 * m : FC0 + 128 * m + 128] = quarters(
                [
                    roll(first, -32 * h),
                    roll(first, -32 - 32 * h),
                    roll(second, 64 - 32 * h),
                    roll(second, 32 - 32 * h),
                ]
            )


def unpack(block, grad_in, w4, wq, wp, small, *outs):
    o_block, o_in, o_gains, o_shifts, o_qkv, o_attn, o_out, o_branch, o_fc, o_fcb, o_proj = outs
    o_block[...] = block[...]
    o_in[...] = grad_in[...]
    o_proj[...] = wp[...]
    for i, o in enumerate((o_gains, o_shifts, o_attn, o_branch)):
        o[...] = small[2 * i : 2 * i + 2, 0:8]
    o_fcb[...] = roll(small[...], -32)[0:1, 0:32]
    lane = lax.broadcasted_iota(jnp.int32, (8, 128), 1)
    for h in range(2):
        o_out[:, h * HALF : (h + 1) * HALF] = w4[h, :, GOUT0 : GOUT0 + HALF]
        for k in range(3):
            for j in range(0, 8, 2):
                c = 128 * (k // 2)
                even, odd = wq[h, j, :, c : c + 128], wq[h, j + 1, :, c : c + 128]
                sh = 64 * (k % 2)
                at = k * D + h * HALF + 64 * j
                o_qkv[:, at : at + 128] = jnp.where(lane < 64, roll(even, -sh), roll(odd, 64 - sh))
    for k in range(32):
        c = GFC0 + 128 * (k // 2)
        o_fc[:, 128 * k : 128 * k + 128] = quarters(
            [
                roll(w4[a % 2, :, c : c + 128], 32 * a - 32 * ((2 * k + a // 2) % 4))
                for a in range(4)
            ]
        )


def kernel(
    w_qkv,
    w_out,
    w_fc,
    gains,
    shifts,
    attn_biases,
    branch_biases,
    fc_bias,
    tokens,
    cot,
    wproj,
    o_block,
    o_in,
    o_w4,
    o_wq,
    o_wp,
    o_small,
    *scratch,
):
    names = list(SCRATCH)
    r = dict(zip(names, scratch[: len(names)]))
    wpack = r["pack"]
    stages = scratch[len(names) :]
    r["dkv"] = r["sbuf"].at[:, 0 : 2 * HEAD]
    r["dh1"] = r["outp"]
    r["dmid"] = r["part"]
    r["gos"] = r["wor"].at[:, :, :, :, :, 0:HALF]
    r["dqt"] = r["ot"]
    dp, sq = lax.axis_index("dp"), lax.axis_index("seq")
    core = lax.rem(sq, 2)
    me = dict(
        x=lax.div(dp, 2),
        y=lax.div(sq, 4),
        z=lax.rem(lax.div(sq, 2), 2) * 2 + lax.rem(dp, 2),
    )
    my, mz = me["y"], lax.div(me["z"], 2)
    j_me = lax.div(sq, 2)
    partner = (dp, sq + 1 - 2 * core)

    def seq_peer(t):
        jj = lax.rem(j_me + t, 8)
        return jj, (dp, jj * 2 + core)

    def dp_peer(t):
        ii = lax.rem(dp + t, 8)
        return ii, (ii, sq)

    peers = [partner, dev(shift(me, "z", 2 * lax.rem(me["z"], 2) - 1), core)]
    for t in range(1, 8):
        peers += [seq_peer(t)[1], dp_peer(t)[1]]
    bar = pltpu.get_barrier_semaphore()
    for t in peers:
        pl.semaphore_signal(bar, inc=1, device_id=t, device_id_type=MESH)
    vectors = (gains, shifts, attn_biases, branch_biases)
    pack(wpack, r["tiny"], w_qkv, w_out, w_fc, vectors, fc_bias)
    pl.semaphore_wait(bar, len(peers))

    def sems(name):
        return r[name + "_s"], r[name + "_r"]

    def pair(src, dst, i):
        return remote_copy(src, dst, sems("px"), i, partner)

    mine_rows = pl.ds(pl.multiple_of(core * 128, 128), 128)
    their_rows = pl.ds(pl.multiple_of(128 - core * 128, 128), 128)
    half0 = pl.multiple_of(core * HALF, HALF)
    half1 = pl.multiple_of(HALF - core * HALF, HALF)
    own = (me["x"], lax.rem(me["z"], 2), me["y"], mz)

    def tok(jj):
        return pl.ds(pl.multiple_of(jj * T, T), T)

    class Swap:
        def __init__(self, name, k, peer, at, send, land):
            self.name, self.k, self.peer, self.at = name, k, peer, at
            self.send, self.land = send, land

        def copy(self, t):
            pp, to = self.peer(t)
            return remote_copy(
                self.send(pp), self.land(self.at), sems(self.name), self.k * 8 + t, to
            )

        def start(self):
            for t in range(1, 8):
                self.copy(t).start()

        def wait(self):
            for t in range(1, 8):
                pp = lax.rem(self.at + 8 - t, 8)
                remote_copy(
                    self.send(pp), self.land(pp), sems(self.name), self.k * 8 + t, partner
                ).wait_recv()

        def drain(self):
            for t in range(1, 8):
                self.copy(t).wait_send()

    def seq_swap(k, send, land):
        return Swap("a2a", k, seq_peer, j_me, send, land)

    def dp_swap(k, send, land):
        return Swap("dp", k, dp_peer, dp, send, land)

    px_w = pair(wpack.at[1 - core], r["wrecv"], 0)
    px_w.start()

    lc = [
        pltpu.make_async_copy(tokens, r["x"].at[mine_rows], r["loc"].at[1]),
        pltpu.make_async_copy(cot, r["dy"].at[mine_rows], r["loc"].at[2]),
        pltpu.make_async_copy(wproj, r["wp"].at[own], r["loc"].at[3]),
    ]
    for c in lc:
        c.start()
    px_x = pair(tokens, r["x"].at[mine_rows], 1)
    px_dy = pair(cot, r["dy"].at[mine_rows], 2)

    px_w.wait_recv()
    mine, theirs = wpack[core], r["wrecv"][...]
    first = jnp.where(core == 0, mine, theirs)
    second = jnp.where(core == 0, theirs, mine)
    r["w4"][own] = jnp.concatenate([first, second], axis=0).astype(BF16)
    for c in lc:
        c.wait()

    def gathers(table, base):
        out = []
        for i, (name, c0, n, rot) in enumerate(table):
            out.append(Gather(me, core, r[name], c0, n, rot, sems("ag"), (base + i) * 12))
        return out

    ga = gathers(GATHER_A, 0)
    gb = gathers(GATHER_B, 3)
    gc = gathers(GATHER_C, 6)
    for g in ga + gb + gc:
        g.start(0)
    px_x.start()
    px_dy.start()
    for g in ga + gb + gc:
        g.forward(0)
    for g in ga:
        g.finish(0)
        g.start(1)
    for g in gb + gc:
        g.finish(0)
        g.start(1)
    for g in ga:
        g.forward(1)
    for g in ga:
        g.finish(1)
        g.start(2)
    for g in gb + gc:
        g.forward(1)
    for g in ga:
        g.forward(2)
    px_x.wait_recv()
    for g in ga:
        g.finish(2)
    for g in gb:
        g.finish(1)
        g.start(2)

    lane = lax.broadcasted_iota(jnp.int32, (8, 128), 1)
    vec_t = [jnp.zeros((8, 128), F32) for _ in range(8)]
    fcb_t = [jnp.zeros((8, 128), F32) for _ in range(16)]
    for p in range(64):
        tile = r["w4"][
            p // 16, (p // 8) % 2, (p // 2) % 4, p % 2, :, SMALL0 : SMALL0 + 128
        ].astype(F32)
        lo, hi = tile[0:8], tile[8:16]
        at = 16 * (p % 8)
        both = jnp.where(lane < 8, lo, 0.0) + pltpu.roll(jnp.where(lane < 8, hi, 0.0), 8, 1)
        vec_t[p // 8] = vec_t[p // 8] + (pltpu.roll(both, at, 1) if at else both)
        fc = jnp.where(core == 0, lo, hi)
        fc = jnp.where((lane >= 32) & (lane < 64), fc, 0.0)
        sh = (32 * (p % 4) - 32) % 128
        fcb_t[p // 4] = fcb_t[p // 4] + (pltpu.roll(fc, sh, 1) if sh else fc)
    for k in range(8):
        r["vec"][:, 128 * k : 128 * k + 128] = vec_t[k]
    for k in range(16):
        r["fcb"][:, 128 * k : 128 * k + 128] = fcb_t[k]

    def vrow(i):
        return r["vec"][i : i + 1, :]

    def ln1(rows, c):
        xhat, _ = norm_stats(r["x"][rows, :].astype(F32))
        r["h1"][rows, :] = (xhat * vrow(0) + vrow(2)).astype(BF16)
        return c

    rows_loop(T, 128, ln1)
    for k in range(3):
        w = r["w4"][:, :, :, :, :, k * HALF : (k + 1) * HALF].reshape(D, HALF)
        v = nn(r["h1"][...], w)
        if k == 0:
            v = v + r["vec"][4:5, pl.ds(half0, HALF)]
        if k == 2:
            v = v + r["vec"][5:6, pl.ds(half0, HALF)]
        r["qkvs"][k] = v.T.astype(BF16).reshape(8, HEAD, T)
    qkv_swap = seq_swap(0, lambda j: r["qkvs"].at[:, j], lambda j: r["qkvt"].at[:, :, tok(j)])
    qkv_swap.start()
    r["qkvt"][:, :, tok(j_me)] = r["qkvs"][:, j_me]
    for g in gc:
        g.finish(1)
    for g in gb:
        g.forward(2)
    for g in gc:
        g.start(2)

    def hcopy(src, dst, i, axis, d):
        return remote_copy(src, dst, sems("xg"), i, dev(shift(me, axis, d), core))

    def hrows(yy, zz, row, n):
        return r["hs"].at[yy, zz, core, pl.ds(row, n)]

    def h_from(yy, zz, row, n, i):
        ref = hrows(yy, zz, row, n)
        hcopy(ref, ref, i, "y", 1).wait_recv()

    every = slice(None)
    ym, yp, opposite = mod4(my - 1), mod4(my + 1), mod4(my + 2)
    h_z = hcopy(hrows(my, mz, 0, 128), hrows(my, mz, 0, 128), 0, "z", 2)
    h_y = [
        hcopy(hrows(my, every, 0, 128), hrows(my, every, 0, 128), 1 + way(d), "y", d)
        for d in (1, -1)
    ]
    h_f = [
        hcopy(hrows(ym, every, 0, 64), hrows(ym, every, 0, 64), 3, "y", 1),
        hcopy(hrows(yp, every, 64, 64), hrows(yp, every, 64, 64), 4, "y", -1),
    ]
    h1s = r["hs"].reshape(LEN, D)
    k_t, v_t = r["qkvt"].at[1], r["qkvt"].at[2]
    qkv_swap.wait()

    r["qz"][0:HEAD, :] = r["qkvt"][0]
    r["qz"][HEAD:, :] = jnp.zeros((HEAD, LEN), BF16)

    def to_rows(ref, parts):
        def one(i, c):
            cols = pl.ds(pl.multiple_of(i * JB, JB), JB)
            stacked = jnp.concatenate([p(cols) for p in parts], axis=0).astype(F32)
            ref[cols, :] = stacked.T.astype(BF16)
            return c

        lax.fori_loop(0, LEN // JB, one, 0)

    to_rows(r["kv"], [lambda cols: k_t[:, cols], lambda cols: v_t[:, cols]])

    row_i = lax.broadcasted_iota(jnp.int32, (JB, IB), 0)
    col_i = lax.broadcasted_iota(jnp.int32, (JB, IB), 1)

    def jcols(jb):
        return pl.ds(pl.multiple_of(jb * JB, JB), JB)

    def attend(ib, c):
        icols = pl.ds(pl.multiple_of(ib * IB, IB), IB)
        q = r["qz"][:, icols]
        nfull = lax.div(ib * IB, JB)

        def fold_max(s):
            return jnp.max(s.reshape(JB // 8, 8, IB), axis=0)

        def scores(jb, m):
            s = nn(r["kv"][jcols(jb), :], q)
            r["sbuf"][jcols(jb), :] = s
            return jnp.maximum(m, fold_max(s))

        m = lax.fori_loop(0, nfull, scores, jnp.full((8, IB), LOW, F32))
        s = nn(r["kv"][jcols(nfull), :], q)
        s = jnp.where(nfull * JB + row_i <= ib * IB + col_i, s, LOW)
        r["sbuf"][jcols(nfull), :] = s
        m = jnp.max(jnp.maximum(m, fold_max(s)), axis=0, keepdims=True) * SCALE2

        def weigh(jb, state):
            l, o = state
            p = jnp.exp2(r["sbuf"][jcols(jb), :] * SCALE2 - m)
            l = l + fold8(p)
            return l, o + nn(v_t[:, jcols(jb)], p.astype(BF16))

        l, o = lax.fori_loop(
            0, nfull + 1, weigh, (jnp.zeros((8, IB), F32), jnp.zeros((HEAD, IB), F32))
        )
        l = jnp.sum(l, axis=0, keepdims=True)
        o = o / l
        r["ot"][:, icols] = o
        r["ots"][:, icols] = o.astype(BF16)
        r["lse"][:, icols] = jnp.broadcast_to(m + jnp.log2(l), (8, IB))

        @pl.when(ib == 5)
        def _():
            for g in gc:
                g.forward(2)

        return c

    lax.fori_loop(0, LEN // IB, attend, 0)
    att_swap = seq_swap(1, lambda j: r["ots"].at[:, tok(j)], lambda j: r["attt"].at[j])
    att_swap.start()
    r["attt"][j_me] = r["ots"][:, tok(j_me)]
    for g in gb:
        g.finish(2)
    keep = r["w4"].at[pl.ds(2 * core, 2), :, :, :, :, pl.ds(OUT0, HALF)]
    give = r["w4"].at[pl.ds(2 - 2 * core, 2), :, :, :, :, pl.ds(OUT0, HALF)]
    wor_mine = r["wor"].at[:, :, :, :, :, pl.ds(half0, HALF)]
    px_wo = pair(give, wor_mine, 3)
    px_wo.start()
    lc_wo = pltpu.make_async_copy(keep, wor_mine, r["loc"].at[4])
    lc_wo.start()
    lc_h = pltpu.make_async_copy(r["h1"].at[mine_rows], r["hs"].at[my, mz, core], r["loc"].at[5])
    lc_h.start()
    lc_h.wait()
    h_z.start()
    att_swap.wait()
    lc_wo.wait()
    px_wo.wait_recv()

    att = r["attt"][...].reshape(8 * HEAD, T).astype(F32).T.astype(BF16)
    r["part"][...] = nn(att, r["wor"][...].reshape(HALF, D))
    px_p = pair(r["part"], r["partr"], 4)
    px_p.start()
    px_p.wait()

    def ln2(rows, c):
        mid = r["x"][rows, :].astype(F32) + (r["part"][rows, :] + r["partr"][rows, :] + vrow(6))
        r["middle"][rows, :] = mid
        xhat, _ = norm_stats(mid)
        r["h2"][rows, :] = (xhat * vrow(1) + vrow(3)).astype(BF16)
        return c

    rows_loop(T, 128, ln2)
    r["h2t"][...] = r["h2"][...].astype(F32).T.astype(BF16)
    px_dy.wait_recv()
    h_from(my, 1 - mz, 0, 128, 0)
    for c in h_y:
        c.start()
    for g in gc:
        g.finish(2)

    def ffn(t, c):
        cols = pl.ds(pl.multiple_of(t * 512, 512), 512)
        wf = r["w4"][:, :, :, :, :, pl.ds(pl.multiple_of(FC0 + t * 512, 128), 512)].reshape(D, 512)
        wp = r["wp"][t].reshape(512, D)
        pre = nn(r["h2"][...], wf) + r["fcb"][0:1, cols]
        d_act = nt(r["dy"][...], wp)
        sq_ = pre * pre
        th = jnp.tanh(0.7978845608028654 * (pre + 0.044715 * sq_ * pre))
        act = 0.5 * pre * (1.0 + th)
        slope = 0.5 * (1.0 + th) + 0.5 * pre * (1.0 - th * th) * (
            0.7978845608028654 * (1.0 + 3.0 * 0.044715 * sq_)
        )
        d_pre = (slope * d_act).astype(BF16)
        r["act"][:, cols] = act.astype(BF16)
        r["dpre"][:, cols] = d_pre
        r["sfc"][:, cols] = jnp.broadcast_to(
            jnp.sum(d_pre.astype(F32), axis=0, keepdims=True), (8, 512)
        )

        return c

    lax.fori_loop(0, 4, ffn, 0)

    def ffn_dh(n, c):
        cols = pl.ds(pl.multiple_of(n * 256, 256), 256)
        r["dh"][:, cols] = nt(r["dpre"][...], r["w4"][n, :, :, :, :, FC0:].reshape(256, FFH))
        return c

    lax.fori_loop(0, 4, ffn_dh, 0)
    px_dh = pair(r["dh"], r["dhr"], 5)
    px_dh.start()

    def reduces(table, base, stage_at):
        out = []
        for i, (name, c0, n, rot) in enumerate(table):
            piece = Reduce(me, core, r[name], c0, n, rot, sems("rs"), (base + i) * 12)
            k = (stage_at + i) * 5
            out.append(piece.attach(stages[k : k + 5]))
        return out

    rp = reduces(REDUCE_P, 0, 0)
    rf = reduces(REDUCE_F, 2, 2)
    ro = reduces(REDUCE_O, 6, 6)

    def grad_proj(t, c):
        hi, lo = lax.div(t, 2), lax.rem(t, 2)
        cols = pl.ds(pl.multiple_of(t * 256, 256), 256)
        act_t = r["act"][:, cols].astype(F32).T.astype(BF16)
        r["gp"][hi, lo] = nn(act_t, r["dy"][...]).astype(BF16).reshape(4, 2, 32, D)
        return c

    lax.fori_loop(0, 8, grad_proj, 0)
    for g in rp:
        g.start(0)

    r["sv"][...] = jnp.zeros((8, D), F32)
    px_dh.wait_recv()

    def ln2_back(rows, c):
        dh = r["dh"][rows, :] + r["dhr"][rows, :]
        r["dhr"][rows, :] = dh
        xhat, inv = norm_stats(r["middle"][rows, :])
        d_mid = r["dy"][rows, :].astype(F32) + norm_back(xhat, inv, dh, vrow(1))
        r["dmid"][rows, :] = d_mid
        r["dbr"][rows, :] = d_mid.astype(BF16)
        return c

    rows_loop(T, 128, ln2_back)

    wor = r["wor"][...].reshape(HALF, D)
    r["datt"][...] = nt(wor, r["dbr"][...]).astype(BF16).reshape(8, HEAD, T)

    datt_swap = seq_swap(
        2, lambda j: r["datt"].at[j], lambda j: r["dz"].at[pl.ds(HEAD, HEAD), tok(j)]
    )
    datt_swap.start()
    r["dz"][HEAD:, tok(j_me)] = r["datt"][j_me]
    r["dz"][0:HEAD, :] = jnp.zeros((HEAD, LEN), BF16)

    gout = nn(r["attt"][...].reshape(HALF, T), r["dbr"][...]).astype(BF16)
    left = gout[:, :HALF].reshape(2, 2, 4, 2, 16, HALF)
    right = gout[:, HALF:].reshape(2, 2, 4, 2, 16, HALF)
    go_at = r["g4"].at[pl.ds(2 * core, 2), :, :, :, :, pl.ds(GOUT0, HALF)]
    go_at[...] = jnp.where(core == 0, left, right)
    r["gos"][...] = jnp.where(core == 0, right, left)
    px_go = pair(r["gos"], go_at, 7)
    px_go.start()

    def grad_fc(t, c):
        cols = pl.ds(pl.multiple_of(GFC0 + t * 256, 256), 256)
        r["g4"][:, :, :, :, :, cols] = (
            nn(r["h2t"][...], r["dpre"][:, pl.ds(pl.multiple_of(t * 256, 256), 256)])
            .astype(BF16)
            .reshape(4, 2, 4, 2, 16, 256)
        )
        return c

    lax.fori_loop(0, 8, grad_fc, 0)
    for g in rf:
        g.start(0)
    px_go.wait_recv()
    for g in ro:
        g.start(0)

    def ffn_out(n, c):
        cols = pl.ds(pl.multiple_of(n * 256, 256), 256)
        r["outp"][:, cols] = nn(r["act"][...], r["wp"][:, :, :, :, :, cols].reshape(FFH, 256))
        return c

    lax.fori_loop(0, 4, ffn_out, 0)
    px_out = pair(r["outp"].at[their_rows], r["outr"], 6)
    px_out.start()

    def small2(i, c):
        s1, s2, s3, s4 = c
        rows = pl.ds(pl.multiple_of(core * 128 + i * 128, 128), 128)
        dh = r["dhr"][rows, :]
        xhat, _ = norm_stats(r["middle"][rows, :])
        return (
            s1 + fold8(dh * xhat),
            s2 + fold8(dh),
            s3 + fold8(r["dbr"][rows, :].astype(F32)),
            s4 + fold8(r["dy"][rows, :].astype(F32)),
        )

    zero = jnp.zeros((8, D), F32)
    sums = lax.fori_loop(0, 1, small2, (zero, zero, zero, zero))
    for row, s in zip((1, 3, 6, 7), sums):
        r["sv"][row : row + 1, :] = jnp.sum(s, axis=0, keepdims=True)

    px_out.wait_recv()

    def block_out(i, c):
        rows = pl.ds(pl.multiple_of(core * 128 + i * 128, 128), 128)
        here = pl.ds(pl.multiple_of(i * 128, 128), 128)
        o_block[here, :] = (
            r["middle"][rows, :] + (r["outp"][rows, :] + r["outr"][here, :]) + vrow(7)
        ).astype(BF16)
        return c

    lax.fori_loop(0, 1, block_out, 0)
    px_out.wait_send()

    h_from(ym, every, 0, 128, 1)
    h_f[0].start()
    h_from(yp, every, 0, 128, 2)
    h_f[1].start()
    rf[0].forward(0)
    for g in rp:
        g.forward(0)
    datt_swap.wait()

    to_rows(r["qd"], [lambda cols: r["qz"][0:HEAD, cols], lambda cols: r["dz"][HEAD:, cols]])
    r["rowdot"][...] = jnp.broadcast_to(
        jnp.sum(r["dz"][HEAD:, :].astype(F32) * r["ot"][...], axis=0, keepdims=True), (8, LEN)
    )
    r["dkv"][...] = jnp.zeros((LEN, 2 * HEAD), F32)
    lane_kv = lax.broadcasted_iota(jnp.int32, (JB, 2 * HEAD), 1)

    px_h = pair(r["hs"].at[:, :, core], r["hs"].at[:, :, core], 12)

    def attend_back(ib, c):
        icols = pl.ds(pl.multiple_of(ib * IB, IB), IB)
        q, do = r["qz"][:, icols], r["dz"][:, icols]
        qd = r["qd"][icols, :]
        lse, dot = r["lse"][0:1, icols], r["rowdot"][0:1, icols]
        nfull = lax.div(ib * IB, JB)

        def step(jb, dq, masked):
            kv = r["kv"][jcols(jb), :]
            p = jnp.exp2(nn(kv, q) * SCALE2 - lse)
            if masked:
                p = jnp.where(jb * JB + row_i <= ib * IB + col_i, p, 0.0)
            ds = (p * (nn(kv, do) - dot)).astype(BF16)
            r["dkv"][jcols(jb), :] += jnp.where(
                lane_kv < HEAD, nn(ds, qd), nn(p.astype(BF16), qd)
            )
            return dq + nn(k_t[:, jcols(jb)], ds)

        dq = lax.fori_loop(
            0, nfull, lambda jb, a: step(jb, a, False), jnp.zeros((HEAD, IB), F32)
        )
        r["dqt"][:, icols] = step(nfull, dq, True)

        @pl.when(ib == 6)
        def _():
            h_from(opposite, every, 0, 64, 3)
            h_from(opposite, every, 64, 64, 4)
            px_h.start()

        @pl.when(ib == 1)
        def _():
            for g in rf[1:]:
                g.forward(0)

        @pl.when(ib == 4)
        def _():
            for g in ro:
                g.forward(0)

        return c

    lax.fori_loop(0, LEN // IB, attend_back, 0)

    r["dqkvt"][0] = (r["dqt"][...] * 0.125).astype(BF16)

    def kv_back(jb, c):
        both = r["dkv"][jcols(jb), :].T
        r["dqkvt"][1, :, jcols(jb)] = (both[:HEAD] * 0.125).astype(BF16)
        r["dqkvt"][2, :, jcols(jb)] = both[HEAD:].astype(BF16)
        return c

    lax.fori_loop(0, LEN // JB, kv_back, 0)

    dqkv_swap = seq_swap(3, lambda j: r["dqkvt"].at[:, :, tok(j)], lambda j: r["dqs"].at[:, j])
    dqkv_swap.start()
    r["dqs"][:, j_me] = r["dqkvt"][:, :, tok(j_me)]

    px_h.wait_recv()
    d192 = r["dqkvt"][...].reshape(3 * HEAD, LEN)
    for k in range(4):
        g = nn(d192, h1s[:, 256 * k : 256 * k + 256]).astype(BF16)
        r["gqs"][2 * k] = g[:, :128]
        r["gqs"][2 * k + 1] = g[:, 128:]
    gq_swap = dp_swap(1, lambda i: r["gqs"].at[i], lambda i: r["gqr"].at[i])
    gq_swap.start()
    r["gqr"][dp] = r["gqs"][dp]
    for g in rp + rf:
        g.finish(0)
        g.start(1)
    dqkv_swap.wait()

    for k in range(3):
        d = r["dqs"][k].reshape(HALF, T).astype(F32).T
        if k != 1:
            row = 4 if k == 0 else 5
            r["sv"][row : row + 1, pl.ds(half0, HALF)] = jnp.sum(d, axis=0, keepdims=True)
        w = r["w4"][:, :, :, :, :, k * HALF : (k + 1) * HALF].reshape(D, HALF)
        v = nt(d.astype(BF16), w)
        r["dh1"][...] = v if k == 0 else r["dh1"][...] + v
    px_d1 = pair(r["dh1"].at[their_rows], r["dh1r"], 8)
    px_d1.start()
    for g in ro:
        g.finish(0)
        g.start(1)
    for g in rp + rf:
        g.finish(1)
        g.start(2)
    gq_swap.wait()
    total = r["gqr"][0].astype(F32)
    for i in range(1, 8):
        total = total + r["gqr"][i].astype(F32)
    total = jnp.concatenate([total, jnp.zeros((HEAD, 128), F32)], axis=0)
    r["gqt"][...] = total.T.reshape(8, 16, 256)
    gqt_swap = seq_swap(4, lambda j: r["gqt"].at[j], lambda j: r["finq"].at[j])
    gqt_swap.start()
    r["finq"][j_me] = r["gqt"][j_me]
    px_d1.wait_recv()

    def ln1_back(i, c):
        s1, s2 = c
        rows = pl.ds(pl.multiple_of(core * 128 + i * 128, 128), 128)
        here = pl.ds(pl.multiple_of(i * 128, 128), 128)
        dh = r["dh1"][rows, :] + r["dh1r"][here, :]
        xhat, inv = norm_stats(r["x"][rows, :].astype(F32))
        d_in = r["dmid"][rows, :] + norm_back(xhat, inv, dh, vrow(0))
        o_in[here, :] = d_in.astype(BF16)
        return s1 + fold8(dh * xhat), s2 + fold8(dh)

    sums = lax.fori_loop(0, 1, ln1_back, (zero, zero))
    for row, s in zip((0, 2), sums):
        r["sv"][row : row + 1, :] = jnp.sum(s, axis=0, keepdims=True)

    for i in range(8):
        r["ss"][i, 0:8] = r["sv"][:, 128 * i : 128 * i + 128]
        r["ss"][i, 8:9] = r["sfc"][0:1, 256 * i : 256 * i + 128]
        r["ss"][i, 9:10] = r["sfc"][0:1, 256 * i + 128 : 256 * i + 256]
        r["ss"][i, 10:16] = jnp.zeros((6, 128), F32)
    ss_swap = dp_swap(2, lambda i: r["ss"].at[i], lambda i: r["ssr"].at[i])
    ss_swap.start()
    r["ssr"][dp] = r["ss"][dp]
    for g in ro:
        g.finish(1)
        g.start(2)
    ss_swap.wait()
    r["st"][...] = jnp.sum(r["ssr"][...], axis=0)
    st_swap = seq_swap(5, lambda j: r["st"], lambda j: r["str"].at[j])
    st_swap.start()
    r["str"][j_me] = r["st"][...]

    mine8 = pl.ds(pl.multiple_of(core * 8, 8), 8)
    their8 = pl.ds(pl.multiple_of(8 - core * 8, 8), 8)
    gqt_swap.wait()
    px_q = pair(r["finq"].at[:, their8], o_wq.at[core], 11)
    px_q.start()
    o_wq[core] = r["finq"][:, mine8, :]
    for g in rp + rf + ro:
        tall = g.ref is r["gp"]
        g.finish(2, (o_wp if tall else r["fin"]).at[:, pl.ds(g.c0, g.n)])
    px_f = pair(r["fin"].at[their8], o_w4.at[core], 9)
    px_f.start()
    o_w4[core] = r["fin"][mine8, :]
    st_swap.wait()
    r["fins"][...] = jnp.sum(r["str"][...], axis=0)
    px_s = pair(r["fins"], r["finr"], 10)
    px_s.start()
    px_s.wait_recv()
    total = r["fins"][0:8, :] + r["finr"][0:8, :]
    total = pltpu.roll(total, lax.rem(128 - (16 * j_me + 8 * core), 128), 1)
    fc = jnp.where(lax.div(j_me, 4) == 0, r["fins"][8:9, :], r["fins"][9:10, :])
    fc = pltpu.roll(jnp.broadcast_to(fc, (8, 128)), lax.rem(160 - 32 * lax.rem(j_me, 4), 128), 1)
    o_small[...] = jnp.where(lane < 8, total, fc)
    px_q.wait_recv()
    px_f.wait_recv()

    for g in ga + gb + gc + rp + rf + ro:
        g.drain()
    for g in (qkv_swap, att_swap, datt_swap, dqkv_swap, gq_swap, gqt_swap, ss_swap, st_swap):
        g.drain()
    for c in (px_w, px_x, px_dy, px_wo, px_dh, px_go, px_d1, px_q, px_f, px_s, px_h, h_z, *h_y, *h_f):
        c.wait_send()


def stage_list():
    out = []
    for name, _, n, rot in REDUCE_P + REDUCE_F + REDUCE_O:
        out += Reduce.stage_shapes(ROWS[name], n, rot, BF16)
    return out


def block(*args):
    vm = pl.BlockSpec(memory_space=pltpu.VMEM)
    return pl.pallas_call(
        kernel,
        out_shape=(
            jax.ShapeDtypeStruct((128, D), BF16),
            jax.ShapeDtypeStruct((128, D), BF16),
            jax.ShapeDtypeStruct((2, 8, G4), F32),
            jax.ShapeDtypeStruct((2, 8, 8, 256), F32),
            jax.ShapeDtypeStruct((32, D), F32),
            jax.ShapeDtypeStruct((8, 128), F32),
        ),
        in_specs=[vm] * len(args),
        out_specs=(vm,) * 6,
        scratch_shapes=list(SCRATCH.values()) + stage_list(),
        compiler_params=pltpu.CompilerParams(
            collective_id=0, has_side_effects=True, vmem_limit_bytes=63 * 2**20
        ),
    )(*args)


def outputs(*results):
    vm = pl.BlockSpec(memory_space=pltpu.VMEM)
    vector = jax.ShapeDtypeStruct((2, 8), F32)
    return pl.pallas_call(
        unpack,
        out_shape=(
            jax.ShapeDtypeStruct((128, D), BF16),
            jax.ShapeDtypeStruct((128, D), BF16),
            vector,
            vector,
            jax.ShapeDtypeStruct((8, 3 * D), F32),
            vector,
            jax.ShapeDtypeStruct((8, D), F32),
            vector,
            jax.ShapeDtypeStruct((8, FF), F32),
            jax.ShapeDtypeStruct((1, 32), F32),
            jax.ShapeDtypeStruct((32, D), F32),
        ),
        in_specs=[vm] * len(results),
        out_specs=(vm,) * 11,
    )(*results)


def on_device(
    tokens,
    norm_gains,
    norm_biases,
    w_qkv,
    attn_biases,
    w_out,
    branch_biases,
    w_fc,
    fc_bias,
    w_proj,
    cotangent,
):
    results = block(
        w_qkv,
        w_out,
        w_fc,
        norm_gains,
        norm_biases,
        attn_biases,
        branch_biases,
        fc_bias[None],
        tokens[0],
        cotangent[0],
        w_proj,
    )
    block_out, input_grad, gains, shifts, qkv, attn, out, branch, fc, fcb, proj = outputs(*results)
    return (
        block_out[None],
        input_grad[None],
        gains,
        shifts,
        qkv,
        attn,
        out,
        branch,
        fc,
        fcb[0],
        proj,
    )


def solution(mesh):
    in_specs = (
        P("dp", "seq", None),
        P(None, ("dp", "seq")),
        P(None, ("dp", "seq")),
        P(("dp", "seq"), None),
        P(None, ("dp", "seq")),
        P(("dp", "seq"), None),
        P(None, ("dp", "seq")),
        P(("dp", "seq"), None),
        P(("dp", "seq")),
        P(("dp", "seq"), None),
        P("dp", "seq", None),
    )
    out_specs = (
        P("dp", "seq", None),
        P("dp", "seq", None),
        P(None, ("dp", "seq")),
        P(None, ("dp", "seq")),
        P(("dp", "seq"), None),
        P(None, ("dp", "seq")),
        P(("dp", "seq"), None),
        P(None, ("dp", "seq")),
        P(("dp", "seq"), None),
        P(("dp", "seq")),
        P(("dp", "seq"), None),
    )
    return jax.shard_map(
        on_device, mesh=mesh, in_specs=in_specs, out_specs=out_specs, check_vma=False
    )
```

```python
import functools
import math

import jax
import jax.numpy as jnp
from jax import lax
from jax.experimental import pallas as pl
from jax.experimental.pallas import tpu as pltpu
from jax.sharding import PartitionSpec as P

MESH = pl.DeviceIdType.MESH
BF16 = jnp.bfloat16
F32 = jnp.float32

H = 16
HEAD = 64
D = 1024
FF = 4096
T = 256
LEN = 2048
HALF = D // 2
FFH = FF // 2
EPS = 1e-05
LOW = -1e30
SCALE2 = math.log2(math.e) / math.sqrt(HEAD)

SMALL0 = 3 * HALF
OUT0 = SMALL0 + 128
FC0 = OUT0 + HALF
W4 = FC0 + FFH
GOUT0 = 0
GFC0 = HALF
G4 = GFC0 + FFH

JB = 512
IB = 256

ORDERS = (("x", "y", "z"), ("y", "z", "x"), ("z", "x", "y"))
SIZES = {"x": 4, "y": 4, "z": 4}


def nt(a, b):
    return lax.dot_general(a, b, (((1,), (1,)), ((), ())), preferred_element_type=F32)


def nn(a, b):
    return jnp.dot(a, b, preferred_element_type=F32)


def mod4(v):
    return lax.rem(v + 4, 4)


def dev(co, core):
    x, y, z = co["x"], co["y"], co["z"]
    return (x * 2 + lax.rem(z, 2), y * 4 + lax.div(z, 2) * 2 + core)


def shift(co, axis, d):
    out = dict(co)
    out[axis] = mod4(co[axis] + d)
    return out


def blocks(ref, sel, c0, n):
    s = slice(None)
    x, y, z = sel["x"], sel["y"], sel["z"]
    return ref.at[
        s if x is None else x,
        s if z is None else lax.rem(z, 2),
        s if y is None else y,
        s if z is None else lax.div(z, 2),
        :,
        pl.ds(c0, n),
    ]


def lead_dims(fixed):
    out = []
    if "x" not in fixed:
        out.append(4)
    if "z" not in fixed:
        out.append(2)
    if "y" not in fixed:
        out.append(4)
    if "z" not in fixed:
        out.append(2)
    return tuple(out)


def half_split(n):
    first = ((n // 128) + 1) // 2 * 128
    return ((0, first), (first, n - first))


def way(d):
    return 0 if d > 0 else 1


def remote_copy(src, dst, sems, i, to):
    return pltpu.make_async_remote_copy(
        src_ref=src,
        dst_ref=dst,
        send_sem=sems[0].at[i],
        recv_sem=sems[1].at[i],
        device_id=to,
        device_id_type=MESH,
    )


ring_copy = remote_copy


class Piece:
    def __init__(self, me, core, ref, c0, n, rot, sems, base):
        self.me, self.core, self.ref, self.c0, self.n = me, core, ref, c0, n
        self.order = ORDERS[rot]
        self.sems, self.base = sems, base

    def cols(self, h):
        if h is None:
            return self.c0, self.n
        off, n = half_split(self.n)[h]
        return self.c0 + off, n

    def remote(self, src, dst, ph, st, d):
        to = dev(shift(self.me, self.order[ph], d), self.core)
        return ring_copy(src, dst, self.sems, self.base + ph * 4 + st * 2 + way(d), to)


class Gather(Piece):
    def region(self, ph, off, h):
        sel = {}
        for k, a in enumerate(self.order):
            sel[a] = None if k < ph else (mod4(self.me[a] + off) if k == ph else self.me[a])
        return blocks(self.ref, sel, *self.cols(h))

    direct = (0,)

    def ways1(self):
        return (1, -1) if self.n > 128 else (1,)

    def copy(self, ph, st, d):
        r = self.region(ph, 0, None) if st == 0 else self.region(ph, -d, way(d))
        return self.remote(r, r, ph, st, d)

    def across(self, ph, off):
        r = self.region(ph, off, None)
        return self.remote(r, r, ph, 1, 2)

    def start(self, ph):
        for d in (1, -1):
            self.copy(ph, 0, d).start()
        if ph in self.direct:
            self.across(ph, 0).start()

    def forward(self, ph):
        if ph in self.direct:
            return
        for d in (1, -1):
            r = self.region(ph, -d, None)
            self.remote(r, r, ph, 0, d).wait_recv()
            if d in self.ways1():
                self.copy(ph, 1, d).start()

    def finish(self, ph):
        if ph in self.direct:
            for d in (1, -1):
                r = self.region(ph, -d, None)
                self.remote(r, r, ph, 0, d).wait_recv()
            self.across(ph, 2).wait_recv()
            return
        for d in self.ways1():
            r = self.region(ph, -2 * d, way(d))
            self.remote(r, r, ph, 1, d).wait_recv()

    def drain(self):
        for ph in range(3):
            for d in (1, -1):
                self.copy(ph, 0, d).wait_send()
            if ph in self.direct:
                self.across(ph, 0).wait_send()
            else:
                for d in self.ways1():
                    self.copy(ph, 1, d).wait_send()


class Reduce(Piece):
    def attach(self, stage):
        self.stage = stage
        return self

    @staticmethod
    def stage_shapes(rows, n, rot, dtype):
        (_, n0), (_, n1) = half_split(n)
        lead = [lead_dims(ORDERS[rot][: ph + 1]) for ph in range(3)]
        return [
            pltpu.VMEM(lead[0] + (rows, n0), dtype),
            pltpu.VMEM(lead[0] + (rows, n1), dtype),
            pltpu.VMEM((2,) + lead[0] + (rows, n), dtype),
            pltpu.VMEM((3,) + lead[1] + (rows, n), dtype),
            pltpu.VMEM((3,) + lead[2] + (rows, n), dtype),
        ]

    def region(self, ph, off, h):
        sel = {}
        for k, a in enumerate(self.order):
            sel[a] = self.me[a] if k < ph else (mod4(self.me[a] + off) if k == ph else None)
        return blocks(self.ref, sel, *self.cols(h))

    def copy(self, ph, st, d):
        if st == 0:
            return self.remote(self.region(ph, 2, way(d)), self.stage[way(d)], ph, 0, d)
        return self.remote(self.region(ph, d, None), self.stage[2].at[way(d)], ph, 1, d)

    def straight(self, ph, k):
        d = (1, -1, 2)[k]
        st = 1 if k == 2 else 0
        return self.remote(self.region(ph, d, None), self.stage[2 + ph].at[k], ph, st, d)

    def start(self, ph):
        if ph:
            for k in range(3):
                self.straight(ph, k).start()
        else:
            for d in (1, -1):
                self.copy(0, 0, d).start()

    def add(self, target, sources, lead, wide=False):
        def one(idx):
            total = target[idx].astype(F32) if wide else target[idx]
            for s in sources:
                total = total + s[idx].astype(total.dtype)
            target[idx] = total.astype(target.dtype)

        if not lead:
            one(Ellipsis)
        else:
            lax.fori_loop(0, lead[0], lambda i, c: (one(i), c)[1], 0)

    def forward(self, ph):
        if ph:
            return
        lead = lead_dims(self.order[:1])
        for d in (1, -1):
            self.copy(0, 0, d).wait_recv()
            self.add(self.region(0, d, way(d)), [self.stage[way(d)]], lead)
            self.copy(0, 1, d).start()

    def finish(self, ph, out=None):
        lead = lead_dims(self.order[: ph + 1])
        s = self.stage[2 + ph]
        if ph:
            for k in range(3):
                self.straight(ph, k).wait_recv()
        else:
            for d in (1, -1):
                self.copy(0, 1, d).wait_recv()
        mine = self.region(ph, 0, None)
        arrived = [s.at[k] for k in range(3 if ph else 2)]
        if out is None:
            self.add(mine, arrived, lead, wide=ph > 0)
        else:
            total = mine[...].astype(F32)
            for a in arrived:
                total = total + a[...].astype(F32)
            out[...] = total

    def drain(self):
        for d in (1, -1):
            self.copy(0, 0, d).wait_send()
            self.copy(0, 1, d).wait_send()
        for ph in (1, 2):
            for k in range(3):
                self.straight(ph, k).wait_send()


GATHER_B = (
    ("w4", OUT0, HALF + 256, 0),
    ("w4", FC0 + 256, 768, 1),
    ("w4", FC0 + 1024, 768, 2),
)
GATHER_C = (
    ("w4", FC0 + 1792, 256, 0),
    ("wp", 0, 256, 0),
    ("wp", 256, 384, 1),
    ("wp", 640, 384, 2),
)
GATHER_A = (("w4", 0, HALF, 0), ("w4", HALF, HALF, 1), ("w4", 2 * HALF, HALF + 128, 2))
REDUCE_P = (("gp", 0, HALF, 1), ("gp", HALF, HALF, 2))
REDUCE_F = (
    ("g4", GFC0, 640, 0),
    ("g4", GFC0 + 640, 640, 0),
    ("g4", GFC0 + 1280, 256, 1),
    ("g4", GFC0 + 1536, HALF, 2),
)
REDUCE_O = (("g4", GOUT0, HALF, 0),)
ROWS = {"g4": 16, "gp": 32}


def rows_loop(total, step, body, init=0):
    def one(i, c):
        return body(pl.ds(pl.multiple_of(i * step, step), step), c)

    return lax.fori_loop(0, total // step, one, init)


def fold8(v):
    return jnp.sum(v.reshape(v.shape[0] // 8, 8, v.shape[1]), axis=0)


def norm_stats(v):
    average = jnp.mean(v, axis=-1, keepdims=True)
    centred = v - average
    variance = jnp.mean(centred * centred, axis=-1, keepdims=True)
    inv = lax.rsqrt(variance + EPS)
    return centred * inv, inv


def norm_back(xhat, inv, dh, gain):
    a = dh * gain
    return inv * (
        a - jnp.mean(a, axis=-1, keepdims=True) - xhat * jnp.mean(a * xhat, axis=-1, keepdims=True)
    )


SCRATCH = dict(
    w4=pltpu.VMEM((4, 2, 4, 2, 16, W4), BF16),
    wp=pltpu.VMEM((4, 2, 4, 2, 32, D), BF16),
    g4=pltpu.VMEM((4, 2, 4, 2, 16, G4), BF16),
    gp=pltpu.VMEM((4, 2, 4, 2, 32, D), BF16),
    pack=pltpu.VMEM((2, 8, W4), F32),
    tiny=pltpu.VMEM((2, 8, 128), F32),
    wrecv=pltpu.VMEM((8, W4), F32),
    wor=pltpu.VMEM((2, 2, 4, 2, 16, D), BF16),
    hs=pltpu.VMEM((4, 2, 2, 128, D), BF16),
    h1=pltpu.VMEM((T, D), BF16),
    qkvs=pltpu.VMEM((3, 8, HEAD, T), BF16),
    qkvt=pltpu.VMEM((3, HEAD, LEN), BF16),
    x=pltpu.VMEM((T, D), BF16),
    dy=pltpu.VMEM((T, D), BF16),
    h2=pltpu.VMEM((T, D), BF16),
    h2t=pltpu.VMEM((D, T), BF16),
    vec=pltpu.VMEM((8, D), F32),
    fcb=pltpu.VMEM((8, FFH), F32),
    qz=pltpu.VMEM((2 * HEAD, LEN), BF16),
    dz=pltpu.VMEM((2 * HEAD, LEN), BF16),
    kv=pltpu.VMEM((LEN, 2 * HEAD), BF16),
    qd=pltpu.VMEM((LEN, 2 * HEAD), BF16),
    sbuf=pltpu.VMEM((LEN, IB), F32),
    ot=pltpu.VMEM((HEAD, LEN), F32),
    ots=pltpu.VMEM((HEAD, LEN), BF16),
    lse=pltpu.VMEM((8, LEN), F32),
    rowdot=pltpu.VMEM((8, LEN), F32),
    attt=pltpu.VMEM((8, HEAD, T), BF16),
    act=pltpu.VMEM((T, FFH), BF16),
    dpre=pltpu.VMEM((T, FFH), BF16),
    part=pltpu.VMEM((T, D), F32),
    partr=pltpu.VMEM((T, D), F32),
    middle=pltpu.VMEM((T, D), F32),
    outp=pltpu.VMEM((T, D), F32),
    outr=pltpu.VMEM((T // 2, D), F32),
    dh=pltpu.VMEM((T, D), F32),
    dhr=pltpu.VMEM((T, D), F32),
    dbr=pltpu.VMEM((T, D), BF16),
    datt=pltpu.VMEM((8, HEAD, T), BF16),
    dqkvt=pltpu.VMEM((3, HEAD, LEN), BF16),
    dqs=pltpu.VMEM((3, 8, HEAD, T), BF16),
    dh1r=pltpu.VMEM((T // 2, D), F32),
    gqs=pltpu.VMEM((8, 3 * HEAD, 128), BF16),
    gqr=pltpu.VMEM((8, 3 * HEAD, 128), BF16),
    gqt=pltpu.VMEM((8, 16, 256), F32),
    finq=pltpu.VMEM((8, 16, 256), F32),
    sv=pltpu.VMEM((8, D), F32),
    sfc=pltpu.VMEM((8, FFH), F32),
    ss=pltpu.VMEM((8, 16, 128), F32),
    ssr=pltpu.VMEM((8, 16, 128), F32),
    st=pltpu.VMEM((16, 128), F32),
    str=pltpu.VMEM((8, 16, 128), F32),
    fin=pltpu.VMEM((16, G4), F32),
    fins=pltpu.VMEM((16, 128), F32),
    finr=pltpu.VMEM((16, 128), F32),
    ag_s=pltpu.SemaphoreType.DMA((12 * 10,)),
    ag_r=pltpu.SemaphoreType.DMA((12 * 10,)),
    rs_s=pltpu.SemaphoreType.DMA((12 * 7,)),
    rs_r=pltpu.SemaphoreType.DMA((12 * 7,)),
    xg_s=pltpu.SemaphoreType.DMA((6,)),
    xg_r=pltpu.SemaphoreType.DMA((6,)),
    a2a_s=pltpu.SemaphoreType.DMA((48,)),
    a2a_r=pltpu.SemaphoreType.DMA((48,)),
    dp_s=pltpu.SemaphoreType.DMA((24,)),
    dp_r=pltpu.SemaphoreType.DMA((24,)),
    px_s=pltpu.SemaphoreType.DMA((16,)),
    px_r=pltpu.SemaphoreType.DMA((16,)),
    loc=pltpu.SemaphoreType.DMA((8,)),
)


def roll(v, shift):
    shift %= 128
    return pltpu.roll(v, shift, 1) if shift else v


def quarters(pieces):
    lane = lax.broadcasted_iota(jnp.int32, (8, 128), 1)
    low = jnp.where(lane < 32, pieces[0], pieces[1])
    high = jnp.where(lane < 96, pieces[2], pieces[3])
    return jnp.where(lane < 64, low, high)


def pack(pack_ref, tiny, w_qkv, w_out, w_fc, vectors, fc_bias):
    q, o, f = w_qkv[...].astype(F32), w_out[...].astype(F32), w_fc[...].astype(F32)
    lane = lax.broadcasted_iota(jnp.int32, (8, 128), 1)
    tiny[...] = jnp.zeros((2, 8, 128), F32)
    for i, v in enumerate(vectors):
        tiny[0, 2 * i : 2 * i + 2, 0:8] = v[...].astype(F32)
    tiny[1, 0:1, 0:32] = fc_bias[...].astype(F32)
    small = jnp.where(lane < 8, tiny[0], roll(tiny[1], 32))
    for h in range(2):
        for k in range(3):
            c = k * D + h * HALF
            pack_ref[h, :, k * HALF : (k + 1) * HALF] = q[:, c : c + HALF]
        pack_ref[h, :, SMALL0 : SMALL0 + 128] = small
        pack_ref[h, :, OUT0 : OUT0 + HALF] = o[:, h * HALF : (h + 1) * HALF]
        for m in range(16):
            first = f[:, 256 * m : 256 * m + 128]
            second = f[:, 256 * m + 128 : 256 * m + 256]
            pack_ref[h, :, FC0 + 128 * m : FC0 + 128 * m + 128] = quarters(
                [
                    roll(first, -32 * h),
                    roll(first, -32 - 32 * h),
                    roll(second, 64 - 32 * h),
                    roll(second, 32 - 32 * h),
                ]
            )


def unpack(block, grad_in, w4, wq, wp, small, *outs):
    o_block, o_in, o_gains, o_shifts, o_qkv, o_attn, o_out, o_branch, o_fc, o_fcb, o_proj = outs
    o_block[...] = block[...]
    o_in[...] = grad_in[...]
    o_proj[...] = wp[...]
    for i, o in enumerate((o_gains, o_shifts, o_attn, o_branch)):
        o[...] = small[2 * i : 2 * i + 2, 0:8]
    o_fcb[...] = roll(small[...], -32)[0:1, 0:32]
    lane = lax.broadcasted_iota(jnp.int32, (8, 128), 1)
    for h in range(2):
        o_out[:, h * HALF : (h + 1) * HALF] = w4[h, :, GOUT0 : GOUT0 + HALF]
        for k in range(3):
            for j in range(0, 8, 2):
                c = 128 * (k // 2)
                even, odd = wq[h, j, :, c : c + 128], wq[h, j + 1, :, c : c + 128]
                sh = 64 * (k % 2)
                at = k * D + h * HALF + 64 * j
                o_qkv[:, at : at + 128] = jnp.where(lane < 64, roll(even, -sh), roll(odd, 64 - sh))
    for k in range(32):
        c = GFC0 + 128 * (k // 2)
        o_fc[:, 128 * k : 128 * k + 128] = quarters(
            [
                roll(w4[a % 2, :, c : c + 128], 32 * a - 32 * ((2 * k + a // 2) % 4))
                for a in range(4)
            ]
        )


def kernel(
    w_qkv,
    w_out,
    w_fc,
    gains,
    shifts,
    attn_biases,
    branch_biases,
    fc_bias,
    tokens,
    cot,
    wproj,
    o_block,
    o_in,
    o_w4,
    o_wq,
    o_wp,
    o_small,
    *scratch,
):
    names = list(SCRATCH)
    r = dict(zip(names, scratch[: len(names)]))
    wpack = r["pack"]
    stages = scratch[len(names) :]
    r["dkv"] = r["sbuf"].at[:, 0 : 2 * HEAD]
    r["dh1"] = r["outp"]
    r["dmid"] = r["part"]
    r["gos"] = r["wor"].at[:, :, :, :, :, 0:HALF]
    r["dqt"] = r["ot"]
    dp, sq = lax.axis_index("dp"), lax.axis_index("seq")
    core = lax.rem(sq, 2)
    me = dict(
        x=lax.div(dp, 2),
        y=lax.div(sq, 4),
        z=lax.rem(lax.div(sq, 2), 2) * 2 + lax.rem(dp, 2),
    )
    my, mz = me["y"], lax.div(me["z"], 2)
    j_me = lax.div(sq, 2)
    partner = (dp, sq + 1 - 2 * core)

    def seq_peer(t):
        jj = lax.rem(j_me + t, 8)
        return jj, (dp, jj * 2 + core)

    def dp_peer(t):
        ii = lax.rem(dp + t, 8)
        return ii, (ii, sq)

    peers = [partner, dev(shift(me, "z", 2 * lax.rem(me["z"], 2) - 1), core)]
    for t in range(1, 8):
        peers += [seq_peer(t)[1], dp_peer(t)[1]]
    bar = pltpu.get_barrier_semaphore()
    for t in peers:
        pl.semaphore_signal(bar, inc=1, device_id=t, device_id_type=MESH)
    vectors = (gains, shifts, attn_biases, branch_biases)
    pack(wpack, r["tiny"], w_qkv, w_out, w_fc, vectors, fc_bias)
    pl.semaphore_wait(bar, len(peers))

    def sems(name):
        return r[name + "_s"], r[name + "_r"]

    def pair(src, dst, i):
        return remote_copy(src, dst, sems("px"), i, partner)

    mine_rows = pl.ds(pl.multiple_of(core * 128, 128), 128)
    their_rows = pl.ds(pl.multiple_of(128 - core * 128, 128), 128)
    half0 = pl.multiple_of(core * HALF, HALF)
    half1 = pl.multiple_of(HALF - core * HALF, HALF)
    own = (me["x"], lax.rem(me["z"], 2), me["y"], mz)

    def tok(jj):
        return pl.ds(pl.multiple_of(jj * T, T), T)

    class Swap:
        def __init__(self, name, k, peer, at, send, land):
            self.name, self.k, self.peer, self.at = name, k, peer, at
            self.send, self.land = send, land

        def copy(self, t):
            pp, to = self.peer(t)
            return remote_copy(
                self.send(pp), self.land(self.at), sems(self.name), self.k * 8 + t, to
            )

        def start(self):
            for t in range(1, 8):
                self.copy(t).start()

        def wait(self):
            for t in range(1, 8):
                pp = lax.rem(self.at + 8 - t, 8)
                remote_copy(
                    self.send(pp), self.land(pp), sems(self.name), self.k * 8 + t, partner
                ).wait_recv()

        def drain(self):
            for t in range(1, 8):
                self.copy(t).wait_send()

    def seq_swap(k, send, land):
        return Swap("a2a", k, seq_peer, j_me, send, land)

    def dp_swap(k, send, land):
        return Swap("dp", k, dp_peer, dp, send, land)

    px_w = pair(wpack.at[1 - core], r["wrecv"], 0)
    px_w.start()

    lc = [
        pltpu.make_async_copy(tokens, r["x"].at[mine_rows], r["loc"].at[1]),
        pltpu.make_async_copy(cot, r["dy"].at[mine_rows], r["loc"].at[2]),
        pltpu.make_async_copy(wproj, r["wp"].at[own], r["loc"].at[3]),
    ]
    for c in lc:
        c.start()
    px_x = pair(tokens, r["x"].at[mine_rows], 1)
    px_dy = pair(cot, r["dy"].at[mine_rows], 2)

    px_w.wait_recv()
    mine, theirs = wpack[core], r["wrecv"][...]
    first = jnp.where(core == 0, mine, theirs)
    second = jnp.where(core == 0, theirs, mine)
    r["w4"][own] = jnp.concatenate([first, second], axis=0).astype(BF16)
    for c in lc:
        c.wait()

    def gathers(table, base):
        out = []
        for i, (name, c0, n, rot) in enumerate(table):
            out.append(Gather(me, core, r[name], c0, n, rot, sems("ag"), (base + i) * 12))
        return out

    ga = gathers(GATHER_A, 0)
    for g in ga:
        g.direct = (0, 1)
    gb = gathers(GATHER_B, 3)
    gc = gathers(GATHER_C, 6)
    for g in ga + gb + gc:
        g.start(0)
    px_x.start()
    px_dy.start()
    for g in ga + gb + gc:
        g.forward(0)
    for g in ga:
        g.finish(0)
        g.start(1)
    for g in gb + gc:
        g.finish(0)
        g.start(1)
    for g in ga:
        g.forward(1)
    for g in ga:
        g.finish(1)
        g.start(2)
    for g in gb + gc:
        g.forward(1)
    for g in ga:
        g.forward(2)
    px_x.wait_recv()
    for g in ga:
        g.finish(2)
    for g in gb:
        g.finish(1)
        g.start(2)

    lane = lax.broadcasted_iota(jnp.int32, (8, 128), 1)
    vec_t = [jnp.zeros((8, 128), F32) for _ in range(8)]
    fcb_t = [jnp.zeros((8, 128), F32) for _ in range(16)]
    for p in range(64):
        tile = r["w4"][
            p // 16, (p // 8) % 2, (p // 2) % 4, p % 2, :, SMALL0 : SMALL0 + 128
        ].astype(F32)
        lo, hi = tile[0:8], tile[8:16]
        at = 16 * (p % 8)
        both = jnp.where(lane < 8, lo, 0.0) + pltpu.roll(jnp.where(lane < 8, hi, 0.0), 8, 1)
        vec_t[p // 8] = vec_t[p // 8] + (pltpu.roll(both, at, 1) if at else both)
        fc = jnp.where(core == 0, lo, hi)
        fc = jnp.where((lane >= 32) & (lane < 64), fc, 0.0)
        sh = (32 * (p % 4) - 32) % 128
        fcb_t[p // 4] = fcb_t[p // 4] + (pltpu.roll(fc, sh, 1) if sh else fc)
    for k in range(8):
        r["vec"][:, 128 * k : 128 * k + 128] = vec_t[k]
    for k in range(16):
        r["fcb"][:, 128 * k : 128 * k + 128] = fcb_t[k]

    def vrow(i):
        return r["vec"][i : i + 1, :]

    def ln1(rows, c):
        xhat, _ = norm_stats(r["x"][rows, :].astype(F32))
        r["h1"][rows, :] = (xhat * vrow(0) + vrow(2)).astype(BF16)
        return c

    rows_loop(T, 128, ln1)
    for k in range(3):
        w = r["w4"][:, :, :, :, :, k * HALF : (k + 1) * HALF].reshape(D, HALF)
        v = nn(r["h1"][...], w)
        if k == 0:
            v = v + r["vec"][4:5, pl.ds(half0, HALF)]
        if k == 2:
            v = v + r["vec"][5:6, pl.ds(half0, HALF)]
        r["qkvs"][k] = v.T.astype(BF16).reshape(8, HEAD, T)
    qkv_swap = seq_swap(0, lambda j: r["qkvs"].at[:, j], lambda j: r["qkvt"].at[:, :, tok(j)])
    qkv_swap.start()
    r["qkvt"][:, :, tok(j_me)] = r["qkvs"][:, j_me]
    for g in gc:
        g.finish(1)
    for g in gb:
        g.forward(2)
    for g in gc:
        g.start(2)

    def hcopy(src, dst, i, axis, d):
        return remote_copy(src, dst, sems("xg"), i, dev(shift(me, axis, d), core))

    def hrows(yy, zz, row, n):
        return r["hs"].at[yy, zz, core, pl.ds(row, n)]

    def h_from(yy, zz, row, n, i):
        ref = hrows(yy, zz, row, n)
        hcopy(ref, ref, i, "y", 1).wait_recv()

    every = slice(None)
    ym, yp, opposite = mod4(my - 1), mod4(my + 1), mod4(my + 2)
    h_z = hcopy(hrows(my, mz, 0, 128), hrows(my, mz, 0, 128), 0, "z", 2)
    h_y = [
        hcopy(hrows(my, every, 0, 128), hrows(my, every, 0, 128), 1 + way(d), "y", d)
        for d in (1, -1)
    ]
    h_f = [
        hcopy(hrows(ym, every, 0, 64), hrows(ym, every, 0, 64), 3, "y", 1),
        hcopy(hrows(yp, every, 64, 64), hrows(yp, every, 64, 64), 4, "y", -1),
    ]
    h1s = r["hs"].reshape(LEN, D)
    k_t, v_t = r["qkvt"].at[1], r["qkvt"].at[2]
    qkv_swap.wait()

    r["qz"][0:HEAD, :] = r["qkvt"][0]
    r["qz"][HEAD:, :] = jnp.zeros((HEAD, LEN), BF16)

    def to_rows(ref, parts):
        def one(i, c):
            cols = pl.ds(pl.multiple_of(i * JB, JB), JB)
            stacked = jnp.concatenate([p(cols) for p in parts], axis=0).astype(F32)
            ref[cols, :] = stacked.T.astype(BF16)
            return c

        lax.fori_loop(0, LEN // JB, one, 0)

    to_rows(r["kv"], [lambda cols: k_t[:, cols], lambda cols: v_t[:, cols]])

    row_i = lax.broadcasted_iota(jnp.int32, (JB, IB), 0)
    col_i = lax.broadcasted_iota(jnp.int32, (JB, IB), 1)

    def jcols(jb):
        return pl.ds(pl.multiple_of(jb * JB, JB), JB)

    def attend(ib, c):
        icols = pl.ds(pl.multiple_of(ib * IB, IB), IB)
        q = r["qz"][:, icols]
        nfull = lax.div(ib * IB, JB)

        def fold_max(s):
            return jnp.max(s.reshape(JB // 8, 8, IB), axis=0)

        def scores(jb, m):
            s = nn(r["kv"][jcols(jb), :], q)
            r["sbuf"][jcols(jb), :] = s
            return jnp.maximum(m, fold_max(s))

        m = lax.fori_loop(0, nfull, scores, jnp.full((8, IB), LOW, F32))
        s = nn(r["kv"][jcols(nfull), :], q)
        s = jnp.where(nfull * JB + row_i <= ib * IB + col_i, s, LOW)
        r["sbuf"][jcols(nfull), :] = s
        m = jnp.max(jnp.maximum(m, fold_max(s)), axis=0, keepdims=True) * SCALE2

        def weigh(jb, state):
            l, o = state
            p = jnp.exp2(r["sbuf"][jcols(jb), :] * SCALE2 - m)
            l = l + fold8(p)
            return l, o + nn(v_t[:, jcols(jb)], p.astype(BF16))

        l, o = lax.fori_loop(
            0, nfull + 1, weigh, (jnp.zeros((8, IB), F32), jnp.zeros((HEAD, IB), F32))
        )
        l = jnp.sum(l, axis=0, keepdims=True)
        o = o / l
        r["ot"][:, icols] = o
        r["ots"][:, icols] = o.astype(BF16)
        r["lse"][:, icols] = jnp.broadcast_to(m + jnp.log2(l), (8, IB))

        @pl.when(ib == 5)
        def _():
            for g in gc:
                g.forward(2)

        return c

    lax.fori_loop(0, LEN // IB, attend, 0)
    att_swap = seq_swap(1, lambda j: r["ots"].at[:, tok(j)], lambda j: r["attt"].at[j])
    att_swap.start()
    r["attt"][j_me] = r["ots"][:, tok(j_me)]
    for g in gb:
        g.finish(2)
    keep = r["w4"].at[pl.ds(2 * core, 2), :, :, :, :, pl.ds(OUT0, HALF)]
    give = r["w4"].at[pl.ds(2 - 2 * core, 2), :, :, :, :, pl.ds(OUT0, HALF)]
    wor_mine = r["wor"].at[:, :, :, :, :, pl.ds(half0, HALF)]
    px_wo = pair(give, wor_mine, 3)
    px_wo.start()
    lc_wo = pltpu.make_async_copy(keep, wor_mine, r["loc"].at[4])
    lc_wo.start()
    lc_h = pltpu.make_async_copy(r["h1"].at[mine_rows], r["hs"].at[my, mz, core], r["loc"].at[5])
    lc_h.start()
    lc_h.wait()
    h_z.start()
    att_swap.wait()
    lc_wo.wait()
    px_wo.wait_recv()

    att = r["attt"][...].reshape(8 * HEAD, T).astype(F32).T.astype(BF16)
    r["part"][...] = nn(att, r["wor"][...].reshape(HALF, D))
    px_p = pair(r["part"], r["partr"], 4)
    px_p.start()
    px_p.wait()

    def ln2(rows, c):
        mid = r["x"][rows, :].astype(F32) + (r["part"][rows, :] + r["partr"][rows, :] + vrow(6))
        r["middle"][rows, :] = mid
        xhat, _ = norm_stats(mid)
        r["h2"][rows, :] = (xhat * vrow(1) + vrow(3)).astype(BF16)
        return c

    rows_loop(T, 128, ln2)
    r["h2t"][...] = r["h2"][...].astype(F32).T.astype(BF16)
    px_dy.wait_recv()
    h_from(my, 1 - mz, 0, 128, 0)
    for c in h_y:
        c.start()
    for g in gc:
        g.finish(2)

    def ffn(t, c):
        cols = pl.ds(pl.multiple_of(t * 512, 512), 512)
        wf = r["w4"][:, :, :, :, :, pl.ds(pl.multiple_of(FC0 + t * 512, 128), 512)].reshape(D, 512)
        wp = r["wp"][t].reshape(512, D)
        pre = nn(r["h2"][...], wf) + r["fcb"][0:1, cols]
        d_act = nt(r["dy"][...], wp)
        sq_ = pre * pre
        th = jnp.tanh(0.7978845608028654 * (pre + 0.044715 * sq_ * pre))
        act = 0.5 * pre * (1.0 + th)
        slope = 0.5 * (1.0 + th) + 0.5 * pre * (1.0 - th * th) * (
            0.7978845608028654 * (1.0 + 3.0 * 0.044715 * sq_)
        )
        d_pre = (slope * d_act).astype(BF16)
        r["act"][:, cols] = act.astype(BF16)
        r["dpre"][:, cols] = d_pre
        r["sfc"][:, cols] = jnp.broadcast_to(
            jnp.sum(d_pre.astype(F32), axis=0, keepdims=True), (8, 512)
        )

        return c

    lax.fori_loop(0, 4, ffn, 0)

    def ffn_dh(n, c):
        cols = pl.ds(pl.multiple_of(n * 256, 256), 256)
        r["dh"][:, cols] = nt(r["dpre"][...], r["w4"][n, :, :, :, :, FC0:].reshape(256, FFH))
        return c

    lax.fori_loop(0, 4, ffn_dh, 0)
    px_dh = pair(r["dh"], r["dhr"], 5)
    px_dh.start()

    def reduces(table, base, stage_at):
        out = []
        for i, (name, c0, n, rot) in enumerate(table):
            piece = Reduce(me, core, r[name], c0, n, rot, sems("rs"), (base + i) * 12)
            k = (stage_at + i) * 5
            out.append(piece.attach(stages[k : k + 5]))
        return out

    rp = reduces(REDUCE_P, 0, 0)
    rf = reduces(REDUCE_F, 2, 2)
    ro = reduces(REDUCE_O, 6, 6)

    def grad_proj(t, c):
        hi, lo = lax.div(t, 2), lax.rem(t, 2)
        cols = pl.ds(pl.multiple_of(t * 256, 256), 256)
        act_t = r["act"][:, cols].astype(F32).T.astype(BF16)
        r["gp"][hi, lo] = nn(act_t, r["dy"][...]).astype(BF16).reshape(4, 2, 32, D)
        return c

    lax.fori_loop(0, 8, grad_proj, 0)
    for g in rp:
        g.start(0)

    r["sv"][...] = jnp.zeros((8, D), F32)
    px_dh.wait_recv()

    def ln2_back(rows, c):
        dh = r["dh"][rows, :] + r["dhr"][rows, :]
        r["dhr"][rows, :] = dh
        xhat, inv = norm_stats(r["middle"][rows, :])
        d_mid = r["dy"][rows, :].astype(F32) + norm_back(xhat, inv, dh, vrow(1))
        r["dmid"][rows, :] = d_mid
        r["dbr"][rows, :] = d_mid.astype(BF16)
        return c

    rows_loop(T, 128, ln2_back)

    wor = r["wor"][...].reshape(HALF, D)
    r["datt"][...] = nt(wor, r["dbr"][...]).astype(BF16).reshape(8, HEAD, T)

    datt_swap = seq_swap(
        2, lambda j: r["datt"].at[j], lambda j: r["dz"].at[pl.ds(HEAD, HEAD), tok(j)]
    )
    datt_swap.start()
    r["dz"][HEAD:, tok(j_me)] = r["datt"][j_me]
    r["dz"][0:HEAD, :] = jnp.zeros((HEAD, LEN), BF16)

    gout = nn(r["attt"][...].reshape(HALF, T), r["dbr"][...]).astype(BF16)
    left = gout[:, :HALF].reshape(2, 2, 4, 2, 16, HALF)
    right = gout[:, HALF:].reshape(2, 2, 4, 2, 16, HALF)
    go_at = r["g4"].at[pl.ds(2 * core, 2), :, :, :, :, pl.ds(GOUT0, HALF)]
    go_at[...] = jnp.where(core == 0, left, right)
    r["gos"][...] = jnp.where(core == 0, right, left)
    px_go = pair(r["gos"], go_at, 7)
    px_go.start()

    def grad_fc(t, c):
        cols = pl.ds(pl.multiple_of(GFC0 + t * 256, 256), 256)
        r["g4"][:, :, :, :, :, cols] = (
            nn(r["h2t"][...], r["dpre"][:, pl.ds(pl.multiple_of(t * 256, 256), 256)])
            .astype(BF16)
            .reshape(4, 2, 4, 2, 16, 256)
        )
        return c

    lax.fori_loop(0, 8, grad_fc, 0)
    for g in rf:
        g.start(0)
    px_go.wait_recv()
    for g in ro:
        g.start(0)

    def ffn_out(n, c):
        cols = pl.ds(pl.multiple_of(n * 256, 256), 256)
        r["outp"][:, cols] = nn(r["act"][...], r["wp"][:, :, :, :, :, cols].reshape(FFH, 256))
        return c

    lax.fori_loop(0, 4, ffn_out, 0)
    px_out = pair(r["outp"].at[their_rows], r["outr"], 6)
    px_out.start()

    def small2(i, c):
        s1, s2, s3, s4 = c
        rows = pl.ds(pl.multiple_of(core * 128 + i * 128, 128), 128)
        dh = r["dhr"][rows, :]
        xhat, _ = norm_stats(r["middle"][rows, :])
        return (
            s1 + fold8(dh * xhat),
            s2 + fold8(dh),
            s3 + fold8(r["dbr"][rows, :].astype(F32)),
            s4 + fold8(r["dy"][rows, :].astype(F32)),
        )

    zero = jnp.zeros((8, D), F32)
    sums = lax.fori_loop(0, 1, small2, (zero, zero, zero, zero))
    for row, s in zip((1, 3, 6, 7), sums):
        r["sv"][row : row + 1, :] = jnp.sum(s, axis=0, keepdims=True)

    px_out.wait_recv()

    def block_out(i, c):
        rows = pl.ds(pl.multiple_of(core * 128 + i * 128, 128), 128)
        here = pl.ds(pl.multiple_of(i * 128, 128), 128)
        o_block[here, :] = (
            r["middle"][rows, :] + (r["outp"][rows, :] + r["outr"][here, :]) + vrow(7)
        ).astype(BF16)
        return c

    lax.fori_loop(0, 1, block_out, 0)
    px_out.wait_send()

    h_from(ym, every, 0, 128, 1)
    h_f[0].start()
    h_from(yp, every, 0, 128, 2)
    h_f[1].start()
    rf[0].forward(0)
    for g in rp:
        g.forward(0)
    datt_swap.wait()

    to_rows(r["qd"], [lambda cols: r["qz"][0:HEAD, cols], lambda cols: r["dz"][HEAD:, cols]])
    r["rowdot"][...] = jnp.broadcast_to(
        jnp.sum(r["dz"][HEAD:, :].astype(F32) * r["ot"][...], axis=0, keepdims=True), (8, LEN)
    )
    r["dkv"][...] = jnp.zeros((LEN, 2 * HEAD), F32)
    lane_kv = lax.broadcasted_iota(jnp.int32, (JB, 2 * HEAD), 1)

    px_h = pair(r["hs"].at[:, :, core], r["hs"].at[:, :, core], 12)

    def attend_back(ib, c):
        icols = pl.ds(pl.multiple_of(ib * IB, IB), IB)
        q, do = r["qz"][:, icols], r["dz"][:, icols]
        qd = r["qd"][icols, :]
        lse, dot = r["lse"][0:1, icols], r["rowdot"][0:1, icols]
        nfull = lax.div(ib * IB, JB)

        def step(jb, dq, masked):
            kv = r["kv"][jcols(jb), :]
            p = jnp.exp2(nn(kv, q) * SCALE2 - lse)
            if masked:
                p = jnp.where(jb * JB + row_i <= ib * IB + col_i, p, 0.0)
            ds = (p * (nn(kv, do) - dot)).astype(BF16)
            r["dkv"][jcols(jb), :] += jnp.where(
                lane_kv < HEAD, nn(ds, qd), nn(p.astype(BF16), qd)
            )
            return dq + nn(k_t[:, jcols(jb)], ds)

        dq = lax.fori_loop(
            0, nfull, lambda jb, a: step(jb, a, False), jnp.zeros((HEAD, IB), F32)
        )
        r["dqt"][:, icols] = step(nfull, dq, True)

        @pl.when(ib == 6)
        def _():
            h_from(opposite, every, 0, 64, 3)
            h_from(opposite, every, 64, 64, 4)
            px_h.start()

        @pl.when(ib == 1)
        def _():
            for g in rf[1:]:
                g.forward(0)

        @pl.when(ib == 4)
        def _():
            for g in ro:
                g.forward(0)

        return c

    lax.fori_loop(0, LEN // IB, attend_back, 0)

    r["dqkvt"][0] = (r["dqt"][...] * 0.125).astype(BF16)

    def kv_back(jb, c):
        both = r["dkv"][jcols(jb), :].T
        r["dqkvt"][1, :, jcols(jb)] = (both[:HEAD] * 0.125).astype(BF16)
        r["dqkvt"][2, :, jcols(jb)] = both[HEAD:].astype(BF16)
        return c

    lax.fori_loop(0, LEN // JB, kv_back, 0)

    dqkv_swap = seq_swap(3, lambda j: r["dqkvt"].at[:, :, tok(j)], lambda j: r["dqs"].at[:, j])
    dqkv_swap.start()
    r["dqs"][:, j_me] = r["dqkvt"][:, :, tok(j_me)]

    px_h.wait_recv()
    d192 = r["dqkvt"][...].reshape(3 * HEAD, LEN)
    for k in range(4):
        g = nn(d192, h1s[:, 256 * k : 256 * k + 256]).astype(BF16)
        r["gqs"][2 * k] = g[:, :128]
        r["gqs"][2 * k + 1] = g[:, 128:]
    gq_swap = dp_swap(1, lambda i: r["gqs"].at[i], lambda i: r["gqr"].at[i])
    gq_swap.start()
    r["gqr"][dp] = r["gqs"][dp]
    for g in rp + rf:
        g.finish(0)
        g.start(1)
    dqkv_swap.wait()

    for k in range(3):
        d = r["dqs"][k].reshape(HALF, T).astype(F32).T
        if k != 1:
            row = 4 if k == 0 else 5
            r["sv"][row : row + 1, pl.ds(half0, HALF)] = jnp.sum(d, axis=0, keepdims=True)
        w = r["w4"][:, :, :, :, :, k * HALF : (k + 1) * HALF].reshape(D, HALF)
        v = nt(d.astype(BF16), w)
        r["dh1"][...] = v if k == 0 else r["dh1"][...] + v
    px_d1 = pair(r["dh1"].at[their_rows], r["dh1r"], 8)
    px_d1.start()
    for g in ro:
        g.finish(0)
        g.start(1)
    for g in rp + rf:
        g.finish(1)
        g.start(2)
    gq_swap.wait()
    total = r["gqr"][0].astype(F32)
    for i in range(1, 8):
        total = total + r["gqr"][i].astype(F32)
    total = jnp.concatenate([total, jnp.zeros((HEAD, 128), F32)], axis=0)
    r["gqt"][...] = total.T.reshape(8, 16, 256)
    gqt_swap = seq_swap(4, lambda j: r["gqt"].at[j], lambda j: r["finq"].at[j])
    gqt_swap.start()
    r["finq"][j_me] = r["gqt"][j_me]
    px_d1.wait_recv()

    def ln1_back(i, c):
        s1, s2 = c
        rows = pl.ds(pl.multiple_of(core * 128 + i * 128, 128), 128)
        here = pl.ds(pl.multiple_of(i * 128, 128), 128)
        dh = r["dh1"][rows, :] + r["dh1r"][here, :]
        xhat, inv = norm_stats(r["x"][rows, :].astype(F32))
        d_in = r["dmid"][rows, :] + norm_back(xhat, inv, dh, vrow(0))
        o_in[here, :] = d_in.astype(BF16)
        return s1 + fold8(dh * xhat), s2 + fold8(dh)

    sums = lax.fori_loop(0, 1, ln1_back, (zero, zero))
    for row, s in zip((0, 2), sums):
        r["sv"][row : row + 1, :] = jnp.sum(s, axis=0, keepdims=True)

    for i in range(8):
        r["ss"][i, 0:8] = r["sv"][:, 128 * i : 128 * i + 128]
        r["ss"][i, 8:9] = r["sfc"][0:1, 256 * i : 256 * i + 128]
        r["ss"][i, 9:10] = r["sfc"][0:1, 256 * i + 128 : 256 * i + 256]
        r["ss"][i, 10:16] = jnp.zeros((6, 128), F32)
    ss_swap = dp_swap(2, lambda i: r["ss"].at[i], lambda i: r["ssr"].at[i])
    ss_swap.start()
    r["ssr"][dp] = r["ss"][dp]
    for g in ro:
        g.finish(1)
        g.start(2)
    ss_swap.wait()
    r["st"][...] = jnp.sum(r["ssr"][...], axis=0)
    st_swap = seq_swap(5, lambda j: r["st"], lambda j: r["str"].at[j])
    st_swap.start()
    r["str"][j_me] = r["st"][...]

    mine8 = pl.ds(pl.multiple_of(core * 8, 8), 8)
    their8 = pl.ds(pl.multiple_of(8 - core * 8, 8), 8)
    gqt_swap.wait()
    px_q = pair(r["finq"].at[:, their8], o_wq.at[core], 11)
    px_q.start()
    o_wq[core] = r["finq"][:, mine8, :]
    for g in rp + rf + ro:
        tall = g.ref is r["gp"]
        g.finish(2, (o_wp if tall else r["fin"]).at[:, pl.ds(g.c0, g.n)])
    px_f = pair(r["fin"].at[their8], o_w4.at[core], 9)
    px_f.start()
    o_w4[core] = r["fin"][mine8, :]
    st_swap.wait()
    r["fins"][...] = jnp.sum(r["str"][...], axis=0)
    px_s = pair(r["fins"], r["finr"], 10)
    px_s.start()
    px_s.wait_recv()
    total = r["fins"][0:8, :] + r["finr"][0:8, :]
    total = pltpu.roll(total, lax.rem(128 - (16 * j_me + 8 * core), 128), 1)
    fc = jnp.where(lax.div(j_me, 4) == 0, r["fins"][8:9, :], r["fins"][9:10, :])
    fc = pltpu.roll(jnp.broadcast_to(fc, (8, 128)), lax.rem(160 - 32 * lax.rem(j_me, 4), 128), 1)
    o_small[...] = jnp.where(lane < 8, total, fc)
    px_q.wait_recv()
    px_f.wait_recv()

    for g in ga + gb + gc + rp + rf + ro:
        g.drain()
    for g in (qkv_swap, att_swap, datt_swap, dqkv_swap, gq_swap, gqt_swap, ss_swap, st_swap):
        g.drain()
    for c in (px_w, px_x, px_dy, px_wo, px_dh, px_go, px_d1, px_q, px_f, px_s, px_h, h_z, *h_y, *h_f):
        c.wait_send()


def stage_list():
    out = []
    for name, _, n, rot in REDUCE_P + REDUCE_F + REDUCE_O:
        out += Reduce.stage_shapes(ROWS[name], n, rot, BF16)
    return out


def block(*args):
    vm = pl.BlockSpec(memory_space=pltpu.VMEM)
    return pl.pallas_call(
        kernel,
        out_shape=(
            jax.ShapeDtypeStruct((128, D), BF16),
            jax.ShapeDtypeStruct((128, D), BF16),
            jax.ShapeDtypeStruct((2, 8, G4), F32),
            jax.ShapeDtypeStruct((2, 8, 8, 256), F32),
            jax.ShapeDtypeStruct((32, D), F32),
            jax.ShapeDtypeStruct((8, 128), F32),
        ),
        in_specs=[vm] * len(args),
        out_specs=(vm,) * 6,
        scratch_shapes=list(SCRATCH.values()) + stage_list(),
        compiler_params=pltpu.CompilerParams(
            collective_id=0, has_side_effects=True, vmem_limit_bytes=63 * 2**20
        ),
    )(*args)


def outputs(*results):
    vm = pl.BlockSpec(memory_space=pltpu.VMEM)
    vector = jax.ShapeDtypeStruct((2, 8), F32)
    return pl.pallas_call(
        unpack,
        out_shape=(
            jax.ShapeDtypeStruct((128, D), BF16),
            jax.ShapeDtypeStruct((128, D), BF16),
            vector,
            vector,
            jax.ShapeDtypeStruct((8, 3 * D), F32),
            vector,
            jax.ShapeDtypeStruct((8, D), F32),
            vector,
            jax.ShapeDtypeStruct((8, FF), F32),
            jax.ShapeDtypeStruct((1, 32), F32),
            jax.ShapeDtypeStruct((32, D), F32),
        ),
        in_specs=[vm] * len(results),
        out_specs=(vm,) * 11,
    )(*results)


def on_device(
    tokens,
    norm_gains,
    norm_biases,
    w_qkv,
    attn_biases,
    w_out,
    branch_biases,
    w_fc,
    fc_bias,
    w_proj,
    cotangent,
):
    results = block(
        w_qkv,
        w_out,
        w_fc,
        norm_gains,
        norm_biases,
        attn_biases,
        branch_biases,
        fc_bias[None],
        tokens[0],
        cotangent[0],
        w_proj,
    )
    block_out, input_grad, gains, shifts, qkv, attn, out, branch, fc, fcb, proj = outputs(*results)
    return (
        block_out[None],
        input_grad[None],
        gains,
        shifts,
        qkv,
        attn,
        out,
        branch,
        fc,
        fcb[0],
        proj,
    )


def solution(mesh):
    in_specs = (
        P("dp", "seq", None),
        P(None, ("dp", "seq")),
        P(None, ("dp", "seq")),
        P(("dp", "seq"), None),
        P(None, ("dp", "seq")),
        P(("dp", "seq"), None),
        P(None, ("dp", "seq")),
        P(("dp", "seq"), None),
        P(("dp", "seq")),
        P(("dp", "seq"), None),
        P("dp", "seq", None),
    )
    out_specs = (
        P("dp", "seq", None),
        P("dp", "seq", None),
        P(None, ("dp", "seq")),
        P(None, ("dp", "seq")),
        P(("dp", "seq"), None),
        P(None, ("dp", "seq")),
        P(("dp", "seq"), None),
        P(None, ("dp", "seq")),
        P(("dp", "seq"), None),
        P(("dp", "seq")),
        P(("dp", "seq"), None),
    )
    return jax.shard_map(
        on_device, mesh=mesh, in_specs=in_specs, out_specs=out_specs, check_vma=False
    )
```
